128 devices in a mesh: row: 8 (over y_lo, x), col: 16 (over z, y_hi, core).
Axes of the slice: x: 4, y: 4 (y_hi: 2, y_lo: 2; y = y_hi * 2 + y_lo), z: 4, core: 2. Of those that a mesh axis runs over, the one named last changes fastest.
Arguments:
- latent: bfloat16 [192, 256, 1280], P('row', 'col'), may hold values from -6 to 6
- w_query: bfloat16 [1280, 1280], replicated, may hold values from -0.15625 to 0.15625
- w_key: bfloat16 [1280, 1280], replicated, may hold values from -0.15625 to 0.15625
- w_value: bfloat16 [1280, 1280], replicated, may hold values from -0.15625 to 0.15625
- w_out: bfloat16 [1280, 1280], replicated, may hold values from -0.15625 to 0.15625
- depth_kernel: float32 [9, 1280], replicated, may hold values from -2 to 2
- w_proj: bfloat16 [1280, 1280], replicated, may hold values from -0.15625 to 0.15625
Outputs:
- refined: bfloat16 [192, 256, 1280], P('row', 'col')
The draws below stay inside these ranges and needn't reach their ends.
All inputs are finite; a program needn't handle non-finite values.
Results may differ from the reference program's by a relative error of at most 0.011.
Values may be sent and summed in bfloat16 or wider, within the bound.
No kernel may reach another device: no remote copies, remote signals or barrier semaphores. Data moves between devices by JAX's collectives and lax.ppermute only.
A program may use at most 128 MiB of HBM per device.

```python
import jax
import jax.numpy as jnp
from jax import lax

D = 1280
HEADS = 20
GROUPS = 32
TH = 24
TW = 16
M = 4
H = 192
W = 256


def steps_of(stream_key, dims, cuts, smallest, high):
    level, own = 1.0, jax.random.fold_in(stream_key, 6)
    for dim, parts in cuts:
        draws = jnp.exp(jax.random.uniform(jax.random.fold_in(own, dim), (parts,), jnp.float32, smallest / len(cuts), high / len(cuts)))
        level = level * jnp.repeat(draws, dims[dim] // parts).reshape([-1 if axis == dim else 1 for axis in range(len(dims))])
    return level


def normal_values(key, extent, scale, reach, shards=(), held_as=jnp.bfloat16):
    array = scale * jax.random.normal(key, extent, jnp.float32)
    if shards:
        array = array * steps_of(key, extent, shards, -0.22, 0.18)
    return jnp.clip(array, -reach, reach).astype(held_as)


def setup_inputs(seed: int = 0) -> dict:
    streams_of = jax.random.split(jax.random.key(seed), 8)
    latent = normal_values(streams_of[0], (H, W, D), 1.0, 6.0, ((0, 8), (1, 16)))
    w_query = normal_values(streams_of[1], (D, D), D ** -0.5, 0.15625)
    w_key = normal_values(streams_of[2], (D, D), D ** -0.5, 0.15625)
    w_value = normal_values(streams_of[3], (D, D), D ** -0.5, 0.15625)
    w_out = normal_values(streams_of[4], (D, D), D ** -0.5, 0.15625)
    depth_kernel = normal_values(streams_of[5], (9, D), 9 ** -0.5, 2.0, (), jnp.float32)
    w_proj = normal_values(streams_of[6], (D, D), D ** -0.5, 0.15625)
    return {"latent": latent, "w_query": w_query, "w_key": w_key, "w_value": w_value, "w_out": w_out, "depth_kernel": depth_kernel, "w_proj": w_proj}


def group_norm(values):
    rows, cols, chans = values.shape
    grouped = values.reshape(rows * cols, GROUPS, chans // GROUPS)
    mean = lax.optimization_barrier(jnp.mean(grouped, axis=(0, 2), keepdims=True))
    var = lax.optimization_barrier(jnp.mean(jnp.square(grouped - mean), axis=(0, 2), keepdims=True))
    return ((grouped - mean) / jnp.sqrt(var + 1e-05)).reshape(rows, cols, chans)

def one_head(stacked):
    query = stacked[0].astype(jnp.float32)
    keys = stacked[1].astype(jnp.float32)
    values = stacked[2].astype(jnp.float32)
    scores = jnp.einsum('qd,kd->qk', query, keys) / jnp.sqrt(jnp.float32(query.shape[1]))
    expo = jnp.exp(scores)
    probs = (expo / lax.optimization_barrier(jnp.sum(expo, axis=-1, keepdims=True))).astype(jnp.bfloat16)
    return jnp.einsum('qk,kd->qd', probs.astype(jnp.float32), values)

def refine_block(grid, w_query, w_key, w_value, w_out, depth_kernel, w_proj):
    rows, cols, chans = grid.shape
    cells = rows * cols
    head_size = chans // HEADS
    normed = group_norm(grid.astype(jnp.float32)).astype(jnp.bfloat16).reshape(cells, chans)
    query = jnp.dot(normed, w_query, preferred_element_type=jnp.float32).astype(jnp.bfloat16)
    keys = jnp.dot(normed, w_key, preferred_element_type=jnp.float32).astype(jnp.bfloat16)
    values = jnp.dot(normed, w_value, preferred_element_type=jnp.float32).astype(jnp.bfloat16)
    stacked = jnp.stack([query, keys, values]).reshape(3, cells, HEADS, head_size).transpose(2, 0, 1, 3)
    attended = lax.map(one_head, stacked)
    attended = attended.transpose(1, 0, 2).reshape(cells, chans).astype(jnp.bfloat16)
    hidden = grid.astype(jnp.float32).reshape(cells, chans) + jnp.dot(attended, w_out, preferred_element_type=jnp.float32)
    hidden = hidden.reshape(rows, cols, chans)
    active = jax.nn.silu(group_norm(hidden))
    padded = jnp.pad(active, ((1, 1), (1, 1), (0, 0)))
    mixed = jnp.zeros_like(active)
    for tap_row in range(3):
        for tap_col in range(3):
            mixed = mixed + padded[tap_row:tap_row + rows, tap_col:tap_col + cols] * depth_kernel[3 * tap_row + tap_col]
    mixed = mixed.astype(jnp.bfloat16).reshape(cells, chans)
    result = hidden.reshape(cells, chans) + jnp.dot(mixed, w_proj, preferred_element_type=jnp.float32)
    return result.astype(jnp.bfloat16).reshape(rows, cols, chans)

def reference(latent, w_query, w_key, w_value, w_out, depth_kernel, w_proj):
    weights = (w_query, w_key, w_value, w_out, depth_kernel, w_proj)
    height, width, chans = latent.shape
    tile_rows = height // TH
    tile_cols = width // TW
    count = tile_rows * tile_cols
    padded = jnp.pad(latent, ((M, M), (M, M), (0, 0)))

    def one_tile(index):
        start_row = (index // tile_cols * TH).astype(jnp.int32)
        start_col = (index % tile_cols * TW).astype(jnp.int32)
        window = lax.dynamic_slice(padded, (start_row, start_col, jnp.int32(0)), (TH + 2 * M, TW + 2 * M, chans))
        return refine_block(window, *weights)
    tile_out = lax.map(one_tile, jnp.arange(count, dtype=jnp.int32))

    def accumulate(index, carry):
        total, covers = carry
        start_row = (index // tile_cols * TH).astype(jnp.int32)
        start_col = (index % tile_cols * TW).astype(jnp.int32)
        zero = jnp.int32(0)
        old = lax.dynamic_slice(total, (start_row, start_col, zero), (TH + 2 * M, TW + 2 * M, chans))
        total = lax.dynamic_update_slice(total, old + tile_out[index].astype(jnp.float32), (start_row, start_col, zero))
        seen = lax.dynamic_slice(covers, (start_row, start_col), (TH + 2 * M, TW + 2 * M))
        covers = lax.dynamic_update_slice(covers, seen + 1.0, (start_row, start_col))
        return (total, covers)
    total = jnp.zeros((height + 2 * M, width + 2 * M, chans), jnp.float32)
    covers = jnp.zeros((height + 2 * M, width + 2 * M), jnp.float32)
    total, covers = lax.fori_loop(0, count, accumulate, (total, covers))
    local = (total[M:M + height, M:M + width] / covers[M:M + height, M:M + width, None]).astype(jnp.bfloat16)
    subs = local.reshape(TH, tile_rows, TW, tile_cols, chans).transpose(1, 3, 0, 2, 4)
    subs = subs.reshape(count, TH, TW, chans)
    dilated = lax.map(lambda grid: refine_block(grid, *weights), subs)
    dilated = dilated.reshape(tile_rows, tile_cols, TH, TW, chans).transpose(2, 0, 3, 1, 4).reshape(height, width, chans)
    blended = 0.6 * local.astype(jnp.float32) + 0.4 * dilated.astype(jnp.float32)
    return blended.astype(jnp.bfloat16)
```

```python
import functools

import jax
import jax.numpy as jnp
import numpy as np
from jax import lax
from jax.experimental import pallas as pl
from jax.experimental.pallas import tpu as pltpu
from jax.sharding import PartitionSpec as P

D = 1280
HEADS = 20
HEAD = D // HEADS
GROUPS = 32
GROUP = D // GROUPS
M = 4
TH = 24
TW = 16
WH = TH + 2 * M
WW = TW + 2 * M
OWN = TH * TW
WIN = WH * WW
N_ROW = 8
N_COL = 16
DEV = N_ROW * N_COL
SENT = WH * TW
STRIP = WH * M
PART_H = TH // N_ROW
LANES = 256
BLOCKS = D // LANES
F32 = jnp.float32
BF16 = jnp.bfloat16
HIGH_SUM = 2.0**100
LOW_SUM = 2.0**-100


def window_matrix():
    out = np.zeros((WIN, WIN), np.float32)
    for w in range(WH):
        for c in range(WW):
            if c < M:
                src = SENT + w * M + c
            elif c < M + TW:
                src = w * TW + c - M
            else:
                src = SENT + STRIP + w * M + c - M - TW
            out[w * WW + c, src] = 1
    return out.astype(jnp.bfloat16)


def sending_matrix():
    out = np.zeros((SENT + 2 * STRIP, WIN), np.float32)
    for a in range(N_ROW):
        for k in range(WH // N_ROW):
            w = (a + M) % N_ROW + N_ROW * k
            for b in range(TW):
                out[(a * TW + b) * 4 + k, w * WW + M + b] = 1
            for b in range(M):
                out[SENT + (a * M + b) * 4 + k, w * WW + b] = 1
                out[SENT + STRIP + (a * M + b) * 4 + k, w * WW + M + TW + b] = 1
    return out.astype(jnp.bfloat16)


def returning_matrix():
    out = np.zeros((OWN, OWN), np.float32)
    for r in range(N_ROW):
        for c in range(N_COL):
            for i in range(PART_H):
                out[(r * N_COL + c) * PART_H + i, (r * PART_H + i) * TW + c] = 1
    return out.astype(jnp.bfloat16)


def gathering_matrix(row, col):
    cell = lax.broadcasted_iota(jnp.int32, (OWN, SENT), 0)
    sent = lax.broadcasted_iota(jnp.int32, (OWN, SENT), 1)
    i, c = cell // TW, cell % TW
    r2, c2, k = sent // (N_COL * 4), (sent // 4) % N_COL, sent % 4
    late = (row >= M).astype(jnp.int32)
    hit = jnp.logical_and(c == c2, i == PART_H * r2 + k - late)
    local_row = (i % PART_H) * N_ROW + row
    tile_row = i // PART_H
    two_rows = jnp.logical_or(
        jnp.logical_and(local_row < M, tile_row > 0),
        jnp.logical_and(local_row >= TH - M, tile_row < N_ROW - 1),
    )
    two_cols = jnp.logical_or(
        jnp.logical_and(col < M, c > 0),
        jnp.logical_and(col >= TW - M, c < N_COL - 1),
    )
    scale = jnp.where(two_rows, 0.5, 1.0) * jnp.where(two_cols, 0.5, 1.0)
    return jnp.where(hit, scale, 0.0).astype(BF16)


def dot(a, b):
    return jnp.dot(a, b, preferred_element_type=F32)


def three_parts(row):
    full = jnp.broadcast_to(row, (8, row.shape[1]))
    high = full.astype(BF16).astype(F32)
    rest = full - high
    mid = rest.astype(BF16).astype(F32)
    low = rest - mid
    which = lax.broadcasted_iota(jnp.int32, full.shape, 0)
    parts = jnp.where(which == 0, high, jnp.where(which == 1, mid, jnp.where(which == 2, low, 0.0)))
    return parts.astype(BF16)


def group_mean(row, count):
    chan = lax.broadcasted_iota(jnp.int32, (D, 128), 0)
    first = GROUP * lax.broadcasted_iota(jnp.int32, (D, 128), 1)
    member = jnp.where(jnp.logical_and(chan >= first, chan < first + GROUP), 1.0, 0.0).astype(BF16)
    sums = jnp.sum(dot(three_parts(row), member), axis=0, keepdims=True) * (1.0 / (GROUP * count))
    chan = lax.broadcasted_iota(jnp.int32, (128, D), 1)
    first = GROUP * lax.broadcasted_iota(jnp.int32, (128, D), 0)
    spread = jnp.where(jnp.logical_and(chan >= first, chan < first + GROUP), 1.0, 0.0).astype(BF16)
    return jnp.sum(dot(three_parts(sums), spread), axis=0, keepdims=True)


def group_stats(x_ref, cells):
    mean = group_mean(jnp.sum(x_ref[...], axis=0, keepdims=True), cells)
    var = group_mean(jnp.sum(jnp.square(x_ref[...] - mean), axis=0, keepdims=True), cells)
    return mean, 1.0 / jnp.sqrt(var + 1e-05)


def safe_head(j, pair, half, q_ref, k_ref, v_ref):
    lanes = pl.ds(pair * 128, 128)
    query = q_ref[j, :, lanes]
    lane = lax.broadcasted_iota(jnp.int32, query.shape, 1)
    query = jnp.where((lane // HEAD) == half, query.astype(F32), 0.0).astype(BF16)
    scores = lax.dot_general(
        query, k_ref[j, :, lanes], (((1,), (1,)), ((), ())), preferred_element_type=F32
    )
    expo = jnp.exp(scores - jnp.max(scores, axis=1, keepdims=True))
    probs = (expo / jnp.sum(expo, axis=1, keepdims=True)).astype(BF16)
    return dot(probs, v_ref[j, :, lanes])


def refine(rows, cols, x_ref, weights, buffers, sems, emit):
    cells = rows * cols
    wq, wk, wv, wo, taps, wp = weights
    wq_s, wk_s, wv_s, wo_s, wp_s, normed, q_ref, k_ref, v_ref, att, act, range_ref = buffers
    copies = [
        pltpu.make_async_copy(src, dst, sems.at[i])
        for i, (src, dst) in enumerate(
            ((wq, wq_s), (wk, wk_s), (wv, wv_s), (wo, wo_s), (wp, wp_s))
        )
    ]

    mean, rstd = group_stats(x_ref, cells)
    normed[...] = ((x_ref[...] - mean) * rstd).astype(BF16)
    for copy in copies[:3]:
        copy.wait()

    range_ref[0] = jnp.full((8, 128), 1.0, F32)
    range_ref[1] = jnp.full((8, 128), 1.0, F32)

    def heads(j, carry):
        block = pl.ds(pl.multiple_of(j * LANES, LANES), LANES)
        n = normed[...]
        q_ref[j] = (dot(n, wq_s[:, block]) * (1.0 / 8.0)).astype(BF16)
        k_ref[j] = dot(n, wk_s[:, block]).astype(BF16)
        v_ref[j] = dot(n, wv_s[:, block]).astype(BF16)
        lane = lax.broadcasted_iota(jnp.int32, (cells, 128), 1)
        low, high = range_ref[0], range_ref[1]
        for pair in range(2):
            lanes = slice(pair * 128, pair * 128 + 128)
            query = q_ref[j, :, lanes]
            key = k_ref[j, :, lanes]
            value = jnp.concatenate([v_ref[j, :, lanes], jnp.ones((cells, 128), BF16)], axis=1)
            done = []
            for half in range(2):
                mine = jnp.where((lane < HEAD) == (half == 0), query, jnp.zeros_like(query))
                scores = lax.dot_general(
                    mine, key, (((1,), (1,)), ((), ())), preferred_element_type=F32
                )
                out = dot(jnp.exp(scores).astype(BF16), value)
                total = out[:, 128:]
                low = jnp.minimum(low, jnp.min(total.reshape(cells // 8, 8, 128), axis=0))
                high = jnp.maximum(high, jnp.max(total.reshape(cells // 8, 8, 128), axis=0))
                done.append(out[:, :128] / total)
            att[:, pl.ds(pl.multiple_of(j * LANES + pair * 128, 128), 128)] = jnp.where(
                lane < HEAD, done[0], done[1]
            ).astype(BF16)
        range_ref[0] = low
        range_ref[1] = high
        return carry

    lax.fori_loop(0, BLOCKS, heads, 0)
    in_range = jnp.logical_and(jnp.min(range_ref[0]) > LOW_SUM, jnp.max(range_ref[1]) < HIGH_SUM)

    @pl.when(jnp.logical_not(in_range))
    def _():
        def again(j, carry):
            lane = lax.broadcasted_iota(jnp.int32, (cells, 128), 1)
            for pair in range(2):
                done = [safe_head(j, pair, half, q_ref, k_ref, v_ref) for half in range(2)]
                att[:, pl.ds(pl.multiple_of(j * LANES + pair * 128, 128), 128)] = jnp.where(
                    lane < HEAD, done[0], done[1]
                ).astype(BF16)
            return carry

        lax.fori_loop(0, BLOCKS, again, 0)

    copies[3].wait()
    for j in range(BLOCKS):
        block = slice(j * LANES, j * LANES + LANES)
        x_ref[:, block] += dot(att[...], wo_s[:, block])

    mean, rstd = group_stats(x_ref, cells)
    edge = jnp.zeros((cols, D), F32)
    act[pl.ds(0, cols), :] = edge
    act[pl.ds(cols + cells, cols), :] = edge
    chunk = 4 * cols

    def activate(i, carry):
        at = pl.ds(pl.multiple_of(i * chunk, chunk), chunk)
        value = (x_ref[at, :] - mean) * rstd
        act[pl.ds(pl.multiple_of(i * chunk + cols, 8), chunk), :] = value / (1.0 + jnp.exp(-value))
        return carry

    lax.fori_loop(0, rows // 4, activate, 0)

    def convolve(i, carry):
        spot = lax.broadcasted_iota(jnp.int32, (1, cols, 128), 1)
        start = pl.multiple_of(i * chunk, chunk)
        for t in range(D // 128):
            lanes = slice(t * 128, t * 128 + 128)
            lines = [act[pl.ds(start + d * cols, chunk), lanes] for d in range(3)]
            sums = []
            for dj in range(3):
                part = lines[0] * taps[dj : dj + 1, lanes]
                part = part + lines[1] * taps[3 + dj : 4 + dj, lanes]
                sums.append(part + lines[2] * taps[6 + dj : 7 + dj, lanes])
            left = pltpu.roll(sums[0], 1, 0).reshape(4, cols, 128)
            right = pltpu.roll(sums[2], chunk - 1, 0).reshape(4, cols, 128)
            mixed = sums[1].reshape(4, cols, 128)
            mixed = mixed + jnp.where(spot > 0, left, 0.0) + jnp.where(spot < cols - 1, right, 0.0)
            normed[pl.ds(start, chunk), lanes] = mixed.reshape(chunk, 128).astype(BF16)
        return carry

    lax.fori_loop(0, rows // 4, convolve, 0)
    copies[4].wait()
    for j in range(BLOCKS):
        block = slice(j * LANES, j * LANES + LANES)
        emit(block, x_ref[:, block] + dot(normed[...], wp_s[:, block]))


def start_weights(weights, buffers, sems):
    for i, w in enumerate((0, 1, 2, 3, 5)):
        pltpu.make_async_copy(weights[w], buffers[i], sems.at[i]).start()


def tile_kernel(
    above, own, below, left, right, window, sending, wq, wk, wv, wo, taps, wp,
    main, to_left, to_right, parts, x_ref, out, part_sems, sems, *buffers,
):
    pieces = (above, own, below, left, right)
    copies, start = [], 0
    for i, piece in enumerate(pieces):
        copies.append(
            pltpu.make_async_copy(piece, parts.at[pl.ds(start, piece.shape[0])], part_sems.at[i])
        )
        start += piece.shape[0]
    for copy in copies:
        copy.start()
    weights = (wq, wk, wv, wo, taps, wp)
    start_weights(weights, buffers, sems)
    for copy in copies:
        copy.wait()
    for j in range(BLOCKS):
        block = slice(j * LANES, j * LANES + LANES)
        x_ref[:, block] = dot(window[...], parts[:, block])

    def emit(block, values):
        out[:, block] = values.astype(BF16)

    refine(WH, WW, x_ref, weights, buffers, sems, emit)
    for j in range(BLOCKS):
        block = slice(j * LANES, j * LANES + LANES)
        sent = dot(sending[...], out[:, block]).astype(BF16)
        main[:, block] = sent[:SENT]
        to_left[:, block] = sent[SENT : SENT + STRIP]
        to_right[:, block] = sent[SENT + STRIP :]


def sub_kernel(
    got, gathering, returning, wq, wk, wv, wo, taps, wp,
    result, local, x_ref, out, sems, *buffers,
):
    weights = (wq, wk, wv, wo, taps, wp)
    start_weights(weights, buffers, sems)
    for j in range(BLOCKS):
        block = slice(j * LANES, j * LANES + LANES)
        value = dot(gathering[...], got[:, block]).astype(BF16)
        local[:, block] = value
        x_ref[:, block] = value.astype(F32)

    def emit(block, values):
        dilated = values.astype(BF16).astype(F32)
        out[:, block] = (0.6 * local[:, block].astype(F32) + 0.4 * dilated).astype(BF16)

    refine(TH, TW, x_ref, weights, buffers, sems, emit)
    for j in range(BLOCKS):
        block = slice(j * LANES, j * LANES + LANES)
        result[:, block] = dot(returning[...], out[:, block]).astype(BF16)


def scratch(cells, cols):
    square = pltpu.VMEM((D, D), BF16)
    heads = pltpu.VMEM((BLOCKS, cells, LANES), BF16)
    return [
        pltpu.SemaphoreType.DMA((5,)),
        square, square, square, square, square,
        pltpu.VMEM((cells, D), BF16),
        heads, heads, heads,
        pltpu.VMEM((cells, D), BF16),
        pltpu.VMEM((cells + 2 * cols, D), F32),
        pltpu.VMEM((2, 8, 128), F32),
    ]


ANY = pl.BlockSpec(memory_space=pl.ANY)
VMEM = pl.BlockSpec(memory_space=pltpu.VMEM)
PARAMS = dict(vmem_limit_bytes=56 * 2**20)


def tile_block(above, own, below, left, right, weights):
    rows = jax.ShapeDtypeStruct
    return pl.pallas_call(
        tile_kernel,
        out_shape=(rows((SENT, D), BF16), rows((STRIP, D), BF16), rows((STRIP, D), BF16)),
        in_specs=[ANY] * 5 + [VMEM] * 2 + [ANY] * 4 + [VMEM, ANY],
        out_specs=(VMEM, VMEM, VMEM),
        scratch_shapes=[
            pltpu.VMEM((WIN, D), BF16),
            pltpu.VMEM((WIN, D), F32),
            pltpu.VMEM((WIN, D), BF16),
            pltpu.SemaphoreType.DMA((5,)),
            *scratch(WIN, WW),
        ],
        compiler_params=pltpu.CompilerParams(**PARAMS),
        name="tile_block",
    )(above, own, below, left, right, window_matrix(), sending_matrix(), *weights)


def sub_block(got, gathering, weights):
    return pl.pallas_call(
        sub_kernel,
        out_shape=jax.ShapeDtypeStruct((OWN, D), BF16),
        in_specs=[VMEM] * 3 + [ANY] * 4 + [VMEM, ANY],
        out_specs=VMEM,
        scratch_shapes=[
            pltpu.VMEM((OWN, D), BF16),
            pltpu.VMEM((OWN, D), F32),
            pltpu.VMEM((OWN, D), BF16),
            *scratch(OWN, TW),
        ],
        compiler_params=pltpu.CompilerParams(**PARAMS),
        name="sub_block",
    )(got, gathering, returning_matrix(), *weights)


def shift(value, axis, step):
    count = lax.axis_size(axis)
    pairs = [(i, i + step) for i in range(count) if 0 <= i + step < count]
    return lax.ppermute(value, axis, pairs)


def body(latent, w_query, w_key, w_value, w_out, depth_kernel, w_proj):
    weights = (w_query, w_key, w_value, w_out, depth_kernel, w_proj)
    row, col = lax.axis_index("row"), lax.axis_index("col")
    gathering = gathering_matrix(row, col)
    above = shift(latent[TH - M :], "row", 1)
    below = shift(latent[:M], "row", -1)
    tall = jnp.concatenate([above, latent, below], axis=0)
    left = shift(tall[:, TW - M :].reshape(STRIP, D), "col", 1)
    right = shift(tall[:, :M].reshape(STRIP, D), "col", -1)
    main, to_left, to_right = tile_block(
        above.reshape(M * TW, D), latent.reshape(OWN, D), below.reshape(M * TW, D),
        left, right, weights,
    )
    from_right = shift(to_left, "col", -1).reshape(N_ROW, M, 4, D).astype(F32)
    from_left = shift(to_right, "col", 1).reshape(N_ROW, M, 4, D).astype(F32)
    main = main.reshape(N_ROW, TW, 4, D).astype(F32)
    main = jnp.concatenate(
        [main[:, :M] + from_left, main[:, M : TW - M], main[:, TW - M :] + from_right], axis=1
    ).astype(BF16)
    both = functools.partial(
        lax.all_to_all, axis_name=("row", "col"), split_axis=0, concat_axis=0, tiled=True
    )
    got = both(main.reshape(DEV, 4, D)).reshape(SENT, D)
    refined = sub_block(got, gathering, weights)
    back = both(refined.reshape(DEV, 30, 128)).reshape(N_ROW, N_COL, PART_H, D)
    return back.transpose(2, 0, 1, 3).reshape(TH, TW, D)


def solution(mesh):
    return jax.shard_map(
        body,
        mesh=mesh,
        in_specs=(P("row", "col", None), P(), P(), P(), P(), P(), P()),
        out_specs=P("row", "col", None),
        check_vma=False,
    )
```

```python
import functools

import jax
import jax.numpy as jnp
import numpy as np
from jax import lax
from jax.experimental import pallas as pl
from jax.experimental.pallas import tpu as pltpu
from jax.sharding import PartitionSpec as P

D = 1280
HEADS = 20
HEAD = D // HEADS
GROUPS = 32
GROUP = D // GROUPS
M = 4
TH = 24
TW = 16
WH = TH + 2 * M
WW = TW + 2 * M
OWN = TH * TW
WIN = WH * WW
N_ROW = 8
N_COL = 16
DEV = N_ROW * N_COL
SENT = WH * TW
STRIP = WH * M
SIDE = 2 * STRIP
PART_H = TH // N_ROW
LANES = 256
BLOCKS = D // LANES
F32 = jnp.float32
BF16 = jnp.bfloat16
HIGH_SUM = 2.0**100
LOW_SUM = 2.0**-100


def side_matrix():
    out = np.zeros((SIDE, SIDE), np.float32)
    for w in range(WH):
        for c in range(M):
            out[w * 8 + c, STRIP + w * M + c] = 1
            out[w * 8 + M + c, w * M + c] = 1
    return out.astype(jnp.bfloat16)


def main_matrix():
    out = np.zeros((128, 128), np.float32)
    for b in range(TW):
        for h in range(2):
            for k in range(4):
                out[b * 8 + h * 4 + k, h * 64 + k * TW + b] = 1
    return out.astype(jnp.bfloat16)


def strip_matrix():
    out = np.zeros((64, 64), np.float32)
    for b in range(M):
        for h in range(2):
            for k in range(4):
                out[b * 8 + h * 4 + k, h * 32 + k * 8 + b] = 1
                out[32 + b * 8 + h * 4 + k, h * 32 + k * 8 + M + b] = 1
    return out.astype(jnp.bfloat16)


def gather_matrices():
    out = np.zeros((2, 3, 2, 96, 256), np.float32)
    for late in range(2):
        for kind in range(3):
            for edge in range(2):
                for h in range(2):
                    for i in range(PART_H):
                        for c in range(N_COL):
                            two_cols = (kind == 0 and c > 0) or (kind == 2 and c < N_COL - 1)
                            shared = i == (2 if late else 0) and not edge
                            scale = (0.5 if two_cols else 1.0) * (0.5 if shared else 1.0)
                            to = h * 48 + i * TW + c
                            out[late, kind, edge, to, c * 8 + h * 4 + i + late] = scale
                            if shared:
                                out[late, kind, edge, to, 128 + c * 8 + h * 4 + (0 if late else 3)] = scale
    return out.reshape(6, 2, 96, 256).astype(jnp.bfloat16)


def packing_matrix():
    out = np.zeros((256, 240), np.float32)
    for t in range(5):
        for i in range(PART_H):
            for c in range(N_COL):
                at = 10 * i + 2 * t
                out[(at % 4) // 2 * 128 + c * 8 + at // 4, t * 48 + i * TW + c] = 1
    return out.astype(jnp.bfloat16)


def dot(a, b):
    return jnp.dot(a, b, preferred_element_type=F32)


def three_parts(row):
    full = jnp.broadcast_to(row, (8, row.shape[1]))
    high = full.astype(BF16).astype(F32)
    rest = full - high
    mid = rest.astype(BF16).astype(F32)
    low = rest - mid
    which = lax.broadcasted_iota(jnp.int32, full.shape, 0)
    parts = jnp.where(which == 0, high, jnp.where(which == 1, mid, jnp.where(which == 2, low, 0.0)))
    return parts.astype(BF16)


def group_matrices(member, spread):
    for ref, chan_axis in ((member, 0), (spread, 1)):
        chan = lax.broadcasted_iota(jnp.int32, ref.shape, chan_axis)
        first = GROUP * lax.broadcasted_iota(jnp.int32, ref.shape, 1 - chan_axis)
        inside = jnp.logical_and(chan >= first, chan < first + GROUP)
        ref[...] = jnp.where(inside, 1.0, 0.0).astype(BF16)


def group_mean(row, count, member, spread):
    sums = jnp.sum(dot(three_parts(row), member[...]), axis=0, keepdims=True) * (1.0 / (GROUP * count))
    return jnp.sum(dot(three_parts(sums), spread[...]), axis=0, keepdims=True)


def group_stats(x_ref, member, spread):
    cells = x_ref.shape[0]
    mean = group_mean(jnp.sum(x_ref[...], axis=0, keepdims=True), cells, member, spread)
    var = group_mean(jnp.sum(jnp.square(x_ref[...] - mean), axis=0, keepdims=True), cells, member, spread)
    return mean, 1.0 / jnp.sqrt(var + 1e-05)


def safe_head(j, pair, half, q_ref, k_ref, v_ref):
    lanes = pl.ds(pair * 128, 128)
    query = q_ref[j, :, lanes]
    lane = lax.broadcasted_iota(jnp.int32, query.shape, 1)
    query = jnp.where((lane // HEAD) == half, query.astype(F32), 0.0).astype(BF16)
    scores = lax.dot_general(
        query, k_ref[j, :, lanes], (((1,), (1,)), ((), ())), preferred_element_type=F32
    )
    expo = jnp.exp(scores - jnp.max(scores, axis=1, keepdims=True))
    probs = (expo / jnp.sum(expo, axis=1, keepdims=True)).astype(BF16)
    return dot(probs, v_ref[j, :, lanes])


def weight_copies(weights, buffers, sems):
    wq, wk, wv, wo, _, wp = weights

    def block(i, j):
        src = (wq, wk, wv)[i]
        return pltpu.make_async_copy(
            src.at[:, pl.ds(pl.multiple_of(j * LANES, LANES), LANES)], buffers[i].at[j], sems.at[i, j]
        )

    last = [
        pltpu.make_async_copy(wo, buffers[3], sems.at[3, 0]),
        pltpu.make_async_copy(wp, buffers[4], sems.at[4, 0]),
    ]
    return block, last


def start_block(weights, buffers, sems, j):
    block, _ = weight_copies(weights, buffers, sems)
    for i in range(3):
        block(i, j).start()


def refine(rows, side, x_ref, weights, buffers, sems, emit):
    cells = x_ref.shape[0]
    middle = rows * TW
    taps = weights[4]
    wq_s, wk_s, wv_s, wo_s, wp_s, normed, q_ref, k_ref, v_ref, att, act, range_ref, member, spread = buffers
    weight_block, last = weight_copies(weights, buffers, sems)

    start_block(weights, buffers, sems, 1)
    mean, rstd = group_stats(x_ref, member, spread)
    normed[...] = ((x_ref[...] - mean) * rstd).astype(BF16)
    range_ref[0] = jnp.full((8, 128), 1.0, F32)
    range_ref[1] = jnp.full((8, 128), 1.0, F32)

    def heads(j, carry):
        @pl.when(j < BLOCKS - 2)
        def _():
            start_block(weights, buffers, sems, j + 2)

        @pl.when(j == BLOCKS - 2)
        def _():
            last[0].start()

        @pl.when(j == BLOCKS - 1)
        def _():
            last[1].start()

        for i in range(3):
            weight_block(i, j).wait()
        n = normed[...]
        q_ref[j] = (dot(n, wq_s[j]) * (1.0 / 8.0)).astype(BF16)
        k_ref[j] = dot(n, wk_s[j]).astype(BF16)
        v_ref[j] = dot(n, wv_s[j]).astype(BF16)
        lane = lax.broadcasted_iota(jnp.int32, (cells, 128), 1)
        low, high = range_ref[0], range_ref[1]
        for pair in range(2):
            lanes = slice(pair * 128, pair * 128 + 128)
            query = q_ref[j, :, lanes]
            key = k_ref[j, :, lanes]
            value = jnp.concatenate([v_ref[j, :, lanes], jnp.ones((cells, 128), BF16)], axis=1)
            done = []
            for half in range(2):
                mine = jnp.where((lane < HEAD) == (half == 0), query, jnp.zeros_like(query))
                scores = lax.dot_general(
                    mine, key, (((1,), (1,)), ((), ())), preferred_element_type=F32
                )
                out = dot(jnp.exp(scores).astype(BF16), value)
                total = out[:, 128:]
                low = jnp.minimum(low, jnp.min(total.reshape(cells // 8, 8, 128), axis=0))
                high = jnp.maximum(high, jnp.max(total.reshape(cells // 8, 8, 128), axis=0))
                done.append(out[:, :128] / total)
            att[:, pl.ds(pl.multiple_of(j * LANES + pair * 128, 128), 128)] = jnp.where(
                lane < HEAD, done[0], done[1]
            ).astype(BF16)
        range_ref[0] = low
        range_ref[1] = high
        return carry

    lax.fori_loop(0, BLOCKS, heads, 0)
    in_range = jnp.logical_and(jnp.min(range_ref[0]) > LOW_SUM, jnp.max(range_ref[1]) < HIGH_SUM)

    @pl.when(jnp.logical_not(in_range))
    def _():
        def again(j, carry):
            lane = lax.broadcasted_iota(jnp.int32, (cells, 128), 1)
            for pair in range(2):
                done = [safe_head(j, pair, half, q_ref, k_ref, v_ref) for half in range(2)]
                att[:, pl.ds(pl.multiple_of(j * LANES + pair * 128, 128), 128)] = jnp.where(
                    lane < HEAD, done[0], done[1]
                ).astype(BF16)
            return carry

        lax.fori_loop(0, BLOCKS, again, 0)

    last[0].wait()
    for j in range(BLOCKS):
        block = slice(j * LANES, j * LANES + LANES)
        x_ref[:, block] += dot(att[...], wo_s[:, block])

    mean, rstd = group_stats(x_ref, member, spread)
    second = (rows + 2) * TW
    for start, width in ((0, TW), (second, 8)) if side else ((0, TW),):
        act[pl.ds(start, width), :] = jnp.zeros((width, D), F32)
        act[pl.ds(start + (rows + 1) * width, width), :] = jnp.zeros((width, D), F32)
    half_rstd = 0.5 * rstd
    parts = ((0, 0, TW), (middle, second, 8)) if side else ((0, 0, TW),)

    def activate(i, carry):
        for start, place, width in parts:
            size = 4 * width
            at = pl.ds(pl.multiple_of(start + i * size, size), size)
            half = (x_ref[at, :] - mean) * half_rstd
            to = pl.ds(pl.multiple_of(place + width + i * size, 8), size)
            act[to, :] = half + half * jnp.tanh(half)
        return carry

    lax.fori_loop(0, rows // 4, activate, 0)

    def convolve(i, carry):
        spot = lax.broadcasted_iota(jnp.int32, (4, 8, 128), 1)
        for t in range(D // 128):
            lanes = slice(t * 128, t * 128 + 128)
            weight = [taps[n : n + 1, lanes] for n in range(9)]
            sums = [[], [], []]
            for start, place, width in parts:
                size = 4 * width
                lines = [
                    act[pl.ds(pl.multiple_of(place + i * size + d * width, 8), size), lanes]
                    for d in range(3)
                ]
                for dj in range(3):
                    part = lines[0] * weight[dj] + lines[1] * weight[3 + dj] + lines[2] * weight[6 + dj]
                    part = part.reshape(4, width // 8, 8, 128)
                    sums[dj] += [part[:, n] for n in range(width // 8)]
            left = [pltpu.roll(v, 1, 1) for v in sums[0]]
            right = [pltpu.roll(v, 7, 1) for v in sums[2]]
            count = len(left)
            mixed = []
            for n in range(count):
                before = left[n - 1] if side or n > 0 else jnp.zeros_like(left[n])
                after = right[(n + 1) % count] if side or n < count - 1 else jnp.zeros_like(left[n])
                from_left = jnp.where(spot == 0, before, left[n])
                from_right = jnp.where(spot == 7, after, right[n])
                if n == 2:
                    from_left = jnp.where(spot == M, 0.0, from_left)
                    from_right = jnp.where(spot == M - 1, 0.0, from_right)
                mixed.append(sums[1][n] + from_left + from_right)
            centre = jnp.concatenate([mixed[0][:, None], mixed[1][:, None]], axis=1).reshape(4 * TW, 128)
            normed[pl.ds(pl.multiple_of(i * 4 * TW, 4 * TW), 4 * TW), lanes] = centre.astype(BF16)
            if side:
                normed[pl.ds(pl.multiple_of(middle + i * 32, 32), 32), lanes] = (
                    mixed[2].reshape(32, 128).astype(BF16)
                )
        return carry

    lax.fori_loop(0, rows // 4, convolve, 0)
    last[1].wait()
    for j in range(BLOCKS):
        block = slice(j * LANES, j * LANES + LANES)
        emit(block, x_ref[:, block] + dot(normed[...], wp_s[:, block]))


def halves(value):
    return jnp.concatenate([value[:, : D // 2], value[:, D // 2 :]], axis=0)


def tile_kernel(
    above, own, below, left, right, sides, mains, strips, wq, wk, wv, wo, taps, wp,
    main, to_left, to_right, centre, rims, x_ref, out, out_side, part_sems, sems, *buffers,
):
    copies, start = [], 0
    for i, piece in enumerate((above, own, below)):
        size = piece.shape[0]
        copies.append(pltpu.make_async_copy(piece, centre.at[pl.ds(start, size)], part_sems.at[i]))
        start += size
    copies.append(pltpu.make_async_copy(left, rims.at[pl.ds(0, STRIP)], part_sems.at[3]))
    copies.append(pltpu.make_async_copy(right, rims.at[pl.ds(STRIP, STRIP)], part_sems.at[4]))
    for copy in copies:
        copy.start()
    weights = (wq, wk, wv, wo, taps, wp)
    start_block(weights, buffers, sems, 0)
    group_matrices(buffers[-2], buffers[-1])
    for copy in copies:
        copy.wait()
    x_ref[pl.ds(0, SENT), :] = centre[...].astype(F32)
    x_ref[pl.ds(SENT, SIDE), :] = dot(sides[...], rims[...])

    def emit(block, values):
        rounded = values.astype(BF16)
        out[:, block] = rounded[:SENT]
        out_side[:, block] = rounded[SENT:].astype(F32)

    refine(WH, True, x_ref, weights, buffers, sems, emit)
    for a in range(N_ROW):
        first = (a + M) % N_ROW
        lines = [out[(8 * k + first) * TW : (8 * k + first + 1) * TW, :] for k in range(4)]
        main[a * 128 : a * 128 + 128, :] = dot(
            mains[...], halves(jnp.concatenate(lines, axis=0))
        ).astype(BF16)
        lines = [out_side[(8 * k + first) * 8 : (8 * k + first + 1) * 8, :] for k in range(4)]
        rim = dot(strips[...], halves(jnp.concatenate(lines, axis=0).astype(BF16))).astype(BF16)
        to_right[a * 32 : a * 32 + 32, :] = rim[:32]
        to_left[a * 32 : a * 32 + 32, :] = rim[32:]


def join_kernel(main, from_left, from_right, out):
    for a in range(N_ROW):
        first, last = a * 128, a * 128 + 96
        rim = slice(a * 32, a * 32 + 32)
        out[first : first + 32, :] = (
            main[first : first + 32, :].astype(F32) + from_left[rim, :].astype(F32)
        ).astype(BF16)
        out[first + 32 : last, :] = main[first + 32 : last, :]
        out[last : last + 32, :] = (
            main[last : last + 32, :].astype(F32) + from_right[rim, :].astype(F32)
        ).astype(BF16)


def sub_kernel(
    place, got, gathers, packing, wq, wk, wv, wo, taps, wp,
    result, gather, local, x_ref, out, gather_sem, sems, *buffers,
):
    weights = (wq, wk, wv, wo, taps, wp)
    copy = pltpu.make_async_copy(gathers.at[place[0]], gather, gather_sem)
    copy.start()
    start_block(weights, buffers, sems, 0)
    group_matrices(buffers[-2], buffers[-1])
    late = place[1]
    copy.wait()
    for r in range(N_ROW):
        other = jnp.clip(r + 2 * late - 1, 0, N_ROW - 1)
        edge = 1 - late if r == 0 else late if r == N_ROW - 1 else 0
        cells = jnp.concatenate(
            [got[r * 128 : r * 128 + 128, :], got[pl.ds(pl.multiple_of(other * 128, 128), 128), :]],
            axis=0,
        )
        value = dot(gather[edge], cells).astype(BF16)
        at = slice(r * 48, r * 48 + 48)
        for h in range(2):
            half = slice(h * D // 2, h * D // 2 + D // 2)
            local[at, half] = value[h * 48 : h * 48 + 48]
            x_ref[at, half] = value[h * 48 : h * 48 + 48].astype(F32)

    def emit(block, values):
        dilated = values.astype(BF16).astype(F32)
        out[:, block] = (0.6 * local[:, block].astype(F32) + 0.4 * dilated).astype(BF16)

    refine(TH, False, x_ref, weights, buffers, sems, emit)
    for r in range(N_ROW):
        at = slice(r * 48, r * 48 + 48)
        cells = jnp.concatenate([out[at, t * LANES : t * LANES + LANES] for t in range(BLOCKS)], axis=0)
        packed = dot(packing[...], cells).astype(BF16)
        result[r * 128 : r * 128 + 128, :LANES] = packed[:128]
        result[r * 128 : r * 128 + 128, LANES:] = packed[128:]


def unpack_kernel(got, packing, out):
    for a in range(N_ROW):
        at = slice(a * 128, a * 128 + 128)
        cells = jnp.concatenate([got[at, :LANES], got[at, LANES:]], axis=0)
        value = lax.dot_general(
            packing[...], cells, (((0,), (0,)), ((), ())), preferred_element_type=F32
        ).astype(BF16)
        for t in range(BLOCKS):
            for i in range(PART_H):
                to = (i * N_ROW + a) * TW
                out[to : to + TW, t * LANES : t * LANES + LANES] = value[
                    t * 48 + i * TW : t * 48 + i * TW + TW
                ]


def scratch(cells, padded):
    heads = pltpu.VMEM((BLOCKS, cells, LANES), BF16)
    blocks = pltpu.VMEM((BLOCKS, D, LANES), BF16)
    square = pltpu.VMEM((D, D), BF16)
    return [
        pltpu.SemaphoreType.DMA((5, BLOCKS)),
        blocks, blocks, blocks, square, square,
        pltpu.VMEM((cells, D), BF16),
        heads, heads, heads,
        pltpu.VMEM((cells, D), BF16),
        pltpu.VMEM((padded, D), F32),
        pltpu.VMEM((2, 8, 128), F32),
        pltpu.VMEM((D, 128), BF16),
        pltpu.VMEM((128, D), BF16),
    ]


ANY = pl.BlockSpec(memory_space=pl.ANY)
VMEM = pl.BlockSpec(memory_space=pltpu.VMEM)
PARAMS = dict(vmem_limit_bytes=56 * 2**20)


def tile_block(above, own, below, left, right, weights):
    shape = jax.ShapeDtypeStruct
    return pl.pallas_call(
        tile_kernel,
        out_shape=(
            shape((2 * SENT, D // 2), BF16),
            shape((2 * STRIP, D // 2), BF16),
            shape((2 * STRIP, D // 2), BF16),
        ),
        in_specs=[ANY] * 5 + [VMEM] * 3 + [ANY] * 4 + [VMEM, ANY],
        out_specs=(VMEM, VMEM, VMEM),
        scratch_shapes=[
            pltpu.VMEM((SENT, D), BF16),
            pltpu.VMEM((SIDE, D), BF16),
            pltpu.VMEM((WIN, D), F32),
            pltpu.VMEM((SENT, D), BF16),
            pltpu.VMEM((SIDE, D), F32),
            pltpu.SemaphoreType.DMA((5,)),
            *scratch(WIN, (WH + 2) * WW),
        ],
        compiler_params=pltpu.CompilerParams(**PARAMS),
        name="tile_block",
    )(above, own, below, left, right, side_matrix(), main_matrix(), strip_matrix(), *weights)


def join(main, from_left, from_right):
    return pl.pallas_call(
        join_kernel,
        out_shape=jax.ShapeDtypeStruct(main.shape, BF16),
        in_specs=[VMEM] * 3,
        out_specs=VMEM,
        name="join",
    )(main, from_left, from_right)


def sub_block(place, got, weights):
    return pl.pallas_call(
        sub_kernel,
        out_shape=jax.ShapeDtypeStruct((DEV * 8, 2 * LANES), BF16),
        in_specs=[pl.BlockSpec(memory_space=pltpu.SMEM), VMEM, ANY, VMEM] + [ANY] * 4 + [VMEM, ANY],
        out_specs=VMEM,
        scratch_shapes=[
            pltpu.VMEM((2, 96, 256), BF16),
            pltpu.VMEM((OWN, D), BF16),
            pltpu.VMEM((OWN, D), F32),
            pltpu.VMEM((OWN, D), BF16),
            pltpu.SemaphoreType.DMA,
            *scratch(OWN, (TH + 2) * TW),
        ],
        compiler_params=pltpu.CompilerParams(**PARAMS),
        name="sub_block",
    )(place, got, gather_matrices(), packing_matrix(), *weights)


def unpack(got):
    return pl.pallas_call(
        unpack_kernel,
        out_shape=jax.ShapeDtypeStruct((OWN, D), BF16),
        in_specs=[VMEM] * 2,
        out_specs=VMEM,
        name="unpack",
    )(got, packing_matrix())


def shift(value, axis, step):
    count = lax.axis_size(axis)
    pairs = [(i, i + step) for i in range(count) if 0 <= i + step < count]
    return lax.ppermute(value, axis, pairs)


def body(latent, w_query, w_key, w_value, w_out, depth_kernel, w_proj):
    weights = (w_query, w_key, w_value, w_out, depth_kernel, w_proj)
    row, col = lax.axis_index("row"), lax.axis_index("col")
    late = (row >= M).astype(jnp.int32)
    kind = (col >= M).astype(jnp.int32) + (col >= TW - M).astype(jnp.int32)
    place = jnp.stack([3 * late + kind, late])
    above = shift(latent[TH - M :], "row", 1)
    below = shift(latent[:M], "row", -1)
    tall = jnp.concatenate([above, latent, below], axis=0)
    left = shift(tall[:, TW - M :].reshape(STRIP, D), "col", 1)
    right = shift(tall[:, :M].reshape(STRIP, D), "col", -1)
    main, to_left, to_right = tile_block(
        above.reshape(M * TW, D), latent.reshape(OWN, D), below.reshape(M * TW, D),
        left, right, weights,
    )
    main = join(main, shift(to_right, "col", 1), shift(to_left, "col", -1))
    both = functools.partial(
        lax.all_to_all, axis_name=("row", "col"), split_axis=0, concat_axis=0, tiled=True
    )
    got = both(main.reshape(DEV, 8, D // 2)).reshape(2 * SENT, D // 2)
    refined = sub_block(place, got, weights)
    back = both(refined.reshape(DEV, 8, 2 * LANES)).reshape(DEV * 8, 2 * LANES)
    return unpack(back).reshape(TH, TW, D)


def solution(mesh):
    return jax.shard_map(
        body,
        mesh=mesh,
        in_specs=(P("row", "col", None), P(), P(), P(), P(), P(), P()),
        out_specs=P("row", "col", None),
        check_vma=False,
    )
```

```python
import functools

import jax
import jax.numpy as jnp
import numpy as np
from jax import lax
from jax.experimental import pallas as pl
from jax.experimental.pallas import tpu as pltpu
from jax.sharding import PartitionSpec as P

D = 1280
HEADS = 20
HEAD = D // HEADS
GROUPS = 32
GROUP = D // GROUPS
M = 4
TH = 24
TW = 16
WH = TH + 2 * M
WW = TW + 2 * M
OWN = TH * TW
WIN = WH * WW
N_ROW = 8
N_COL = 16
DEV = N_ROW * N_COL
SENT = WH * TW
STRIP = WH * M
SIDE = 2 * STRIP
PART_H = TH // N_ROW
LANES = 256
BLOCKS = D // LANES
F32 = jnp.float32
BF16 = jnp.bfloat16
HIGH_SUM = 2.0**100
LOW_SUM = 2.0**-100
TILE_MIB = 48
REST_MIB = 14


def side_matrix():
    out = np.zeros((SIDE, SIDE), np.float32)
    for w in range(WH):
        for c in range(M):
            out[w * 8 + c, STRIP + w * M + c] = 1
            out[w * 8 + M + c, w * M + c] = 1
    return out.astype(jnp.bfloat16)


def main_matrix():
    out = np.zeros((128, 128), np.float32)
    for b in range(TW):
        for h in range(2):
            for k in range(4):
                out[b * 8 + h * 4 + k, h * 64 + k * TW + b] = 1
    return out.astype(jnp.bfloat16)


def strip_matrix():
    out = np.zeros((64, 64), np.float32)
    for b in range(M):
        for h in range(2):
            for k in range(4):
                out[b * 8 + h * 4 + k, h * 32 + k * 8 + b] = 1
                out[32 + b * 8 + h * 4 + k, h * 32 + k * 8 + M + b] = 1
    return out.astype(jnp.bfloat16)


def gather_matrices():
    out = np.zeros((2, 3, 2, 96, 256), np.float32)
    for late in range(2):
        for kind in range(3):
            for edge in range(2):
                for h in range(2):
                    for i in range(PART_H):
                        for c in range(N_COL):
                            two_cols = (kind == 0 and c > 0) or (kind == 2 and c < N_COL - 1)
                            shared = i == (2 if late else 0) and not edge
                            scale = (0.5 if two_cols else 1.0) * (0.5 if shared else 1.0)
                            to = h * 48 + i * TW + c
                            out[late, kind, edge, to, c * 8 + h * 4 + i + late] = scale
                            if shared:
                                out[late, kind, edge, to, 128 + c * 8 + h * 4 + (0 if late else 3)] = scale
    return out.reshape(6, 2, 96, 256).astype(jnp.bfloat16)


def packing_matrix():
    out = np.zeros((256, 240), np.float32)
    for t in range(5):
        for i in range(PART_H):
            for c in range(N_COL):
                at = 10 * i + 2 * t
                out[(at % 4) // 2 * 128 + c * 8 + at // 4, t * 48 + i * TW + c] = 1
    return out.astype(jnp.bfloat16)


def dot(a, b):
    return jnp.dot(a, b, preferred_element_type=F32)


def six_parts(first, second):
    shape = (8, first.shape[1])
    which = lax.broadcasted_iota(jnp.int32, shape, 0)
    full = jnp.where(which < 3, jnp.broadcast_to(first, shape), jnp.broadcast_to(second, shape))
    high = full.astype(BF16).astype(F32)
    rest = full - high
    mid = rest.astype(BF16).astype(F32)
    low = rest - mid
    part = jnp.where(which < 3, which, which - 3)
    parts = jnp.where(part == 0, high, jnp.where(part == 1, mid, low))
    return jnp.where(which < 6, parts, 0.0).astype(BF16)


def two_rows(parts):
    return parts[0:1] + parts[1:2] + parts[2:3], parts[3:4] + parts[4:5] + parts[5:6]


def group_matrices(member, spread):
    for ref, chan_axis in ((member, 0), (spread, 1)):
        chan = lax.broadcasted_iota(jnp.int32, ref.shape, chan_axis)
        first = GROUP * lax.broadcasted_iota(jnp.int32, ref.shape, 1 - chan_axis)
        inside = jnp.logical_and(chan >= first, chan < first + GROUP)
        ref[...] = jnp.where(inside, 1.0, 0.0).astype(BF16)


def add_sums(sums, lanes, value):
    tiles = value.reshape(value.shape[0] // 8, 8, value.shape[1])
    sums[0:8, lanes] += jnp.sum(tiles, axis=0)
    sums[8:16, lanes] += jnp.sum(tiles * tiles, axis=0)


def group_stats(x_ref, sums, stats, member, spread):
    scale = 1.0 / (GROUP * x_ref.shape[0])

    def means(first, second):
        first, second = two_rows(dot(six_parts(first, second), member[...]))
        return first * scale, second * scale

    def spread_out(mean, var):
        rstd = 1.0 / jnp.sqrt(jnp.maximum(var, 0.0) + 1e-05)
        mean, rstd = two_rows(dot(six_parts(mean, rstd), spread[...]))
        stats[0:1] = mean
        stats[1:2] = rstd

    total = jnp.sum(sums[0:8], axis=0, keepdims=True)
    mean, square = means(total, jnp.sum(sums[8:16], axis=0, keepdims=True))
    var = square - mean * mean
    spread_out(mean, var)

    @pl.when(jnp.logical_not(jnp.min(var - 0.01 * mean * mean) >= 0.0))
    def _():
        centred = jnp.square(x_ref[...] - stats[0:1])
        _, var = means(total, jnp.sum(centred, axis=0, keepdims=True))
        spread_out(mean, var)

    return stats[0:1], stats[1:2]


def safe_head(j, pair, half, q_ref, k_ref, v_ref):
    lanes = pl.ds(pair * 128, 128)
    query = q_ref[j, :, lanes]
    lane = lax.broadcasted_iota(jnp.int32, query.shape, 1)
    query = jnp.where((lane // HEAD) == half, query.astype(F32), 0.0).astype(BF16)
    scores = lax.dot_general(
        query, k_ref[j, :, lanes], (((1,), (1,)), ((), ())), preferred_element_type=F32
    )
    expo = jnp.exp(scores - jnp.max(scores, axis=1, keepdims=True))
    probs = (expo / jnp.sum(expo, axis=1, keepdims=True)).astype(BF16)
    return dot(probs, v_ref[j, :, lanes])


def weight_copies(weights, buffers, sems):
    wq, wk, wv, wo, _, wp = weights

    def block(i, j):
        src = (wq, wk, wv)[i]
        return pltpu.make_async_copy(
            src.at[:, pl.ds(pl.multiple_of(j * LANES, LANES), LANES)], buffers[i].at[j], sems.at[i, j]
        )

    last = [
        pltpu.make_async_copy(wo, buffers[3], sems.at[3, 0]),
        pltpu.make_async_copy(wp, buffers[4], sems.at[4, 0]),
    ]
    return block, last


def start_block(weights, buffers, sems, j):
    block, _ = weight_copies(weights, buffers, sems)
    for i in range(3):
        block(i, j).start()


def refine(rows, side, x_ref, weights, buffers, sems):
    cells = x_ref.shape[0]
    middle = rows * TW
    taps = weights[4]
    wq_s, wk_s, wv_s, wo_s, wp_s, normed, q_ref, k_ref, v_ref, att, act, range_ref, member, spread, sums, stats = buffers
    weight_block, last = weight_copies(weights, buffers, sems)

    start_block(weights, buffers, sems, 1)
    mean, rstd = group_stats(x_ref, sums, stats, member, spread)
    normed[...] = ((x_ref[...] - mean) * rstd).astype(BF16)
    range_ref[0] = jnp.full((8, 128), 1.0, F32)
    range_ref[1] = jnp.full((8, 128), 1.0, F32)

    def heads(j, carry):
        @pl.when(j < BLOCKS - 2)
        def _():
            start_block(weights, buffers, sems, j + 2)

        @pl.when(j == BLOCKS - 2)
        def _():
            last[0].start()

        @pl.when(j == BLOCKS - 1)
        def _():
            last[1].start()

        for i in range(3):
            weight_block(i, j).wait()
        n = normed[...]
        q_ref[j] = (dot(n, wq_s[j]) * (1.0 / 8.0)).astype(BF16)
        k_ref[j] = dot(n, wk_s[j]).astype(BF16)
        v_ref[j] = dot(n, wv_s[j]).astype(BF16)
        lane = lax.broadcasted_iota(jnp.int32, (cells, 128), 1)
        low, high = range_ref[0], range_ref[1]
        for pair in range(2):
            lanes = slice(pair * 128, pair * 128 + 128)
            query = q_ref[j, :, lanes]
            key = k_ref[j, :, lanes]
            value = jnp.concatenate([v_ref[j, :, lanes], jnp.ones((cells, 128), BF16)], axis=1)
            done = []
            for half in range(2):
                mine = jnp.where((lane < HEAD) == (half == 0), query, jnp.zeros_like(query))
                scores = lax.dot_general(
                    mine, key, (((1,), (1,)), ((), ())), preferred_element_type=F32
                )
                out = dot(jnp.exp(scores).astype(BF16), value)
                total = out[:, 128:]
                low = jnp.minimum(low, jnp.min(total.reshape(cells // 8, 8, 128), axis=0))
                high = jnp.maximum(high, jnp.max(total.reshape(cells // 8, 8, 128), axis=0))
                done.append(out[:, :128] / total)
            att[:, pl.ds(pl.multiple_of(j * LANES + pair * 128, 128), 128)] = jnp.where(
                lane < HEAD, done[0], done[1]
            ).astype(BF16)
        range_ref[0] = low
        range_ref[1] = high
        return carry

    lax.fori_loop(0, BLOCKS, heads, 0)
    in_range = jnp.logical_and(jnp.min(range_ref[0]) > LOW_SUM, jnp.max(range_ref[1]) < HIGH_SUM)

    @pl.when(jnp.logical_not(in_range))
    def _():
        def again(j, carry):
            lane = lax.broadcasted_iota(jnp.int32, (cells, 128), 1)
            for pair in range(2):
                done = [safe_head(j, pair, half, q_ref, k_ref, v_ref) for half in range(2)]
                att[:, pl.ds(pl.multiple_of(j * LANES + pair * 128, 128), 128)] = jnp.where(
                    lane < HEAD, done[0], done[1]
                ).astype(BF16)
            return carry

        lax.fori_loop(0, BLOCKS, again, 0)

    sums[...] = jnp.zeros_like(sums)
    last[0].wait()
    for j in range(BLOCKS):
        block = slice(j * LANES, j * LANES + LANES)
        hidden = x_ref[:, block] + dot(att[...], wo_s[:, block])
        x_ref[:, block] = hidden
        add_sums(sums, block, hidden)

    mean, rstd = group_stats(x_ref, sums, stats, member, spread)
    second = (rows + 2) * TW
    for start, width in ((0, TW), (second, 8)) if side else ((0, TW),):
        act[pl.ds(start, width), :] = jnp.zeros((width, D), F32)
        act[pl.ds(start + (rows + 1) * width, width), :] = jnp.zeros((width, D), F32)
    half_rstd = 0.5 * rstd
    parts = ((0, 0, TW), (middle, second, 8)) if side else ((0, 0, TW),)

    def activate(i, carry):
        for start, place, width in parts:
            size = 4 * width
            at = pl.ds(pl.multiple_of(start + i * size, size), size)
            half = (x_ref[at, :] - mean) * half_rstd
            to = pl.ds(pl.multiple_of(place + width + i * size, 8), size)
            act[to, :] = half + half * jnp.tanh(half)
        return carry

    lax.fori_loop(0, rows // 4, activate, 0)

    def convolve(i, carry):
        spot = lax.broadcasted_iota(jnp.int32, (4, 8, 128), 1)
        for t in range(D // 128):
            lanes = slice(t * 128, t * 128 + 128)
            weight = [taps[n : n + 1, lanes] for n in range(9)]
            sums = [[], [], []]
            for start, place, width in parts:
                size = 4 * width
                lines = [
                    act[pl.ds(pl.multiple_of(place + i * size + d * width, 8), size), lanes]
                    for d in range(3)
                ]
                for dj in range(3):
                    part = lines[0] * weight[dj] + lines[1] * weight[3 + dj] + lines[2] * weight[6 + dj]
                    part = part.reshape(4, width // 8, 8, 128)
                    sums[dj] += [part[:, n] for n in range(width // 8)]
            left = [pltpu.roll(v, 1, 1) for v in sums[0]]
            right = [pltpu.roll(v, 7, 1) for v in sums[2]]
            count = len(left)
            mixed = []
            for n in range(count):
                before = left[n - 1] if side or n > 0 else jnp.zeros_like(left[n])
                after = right[(n + 1) % count] if side or n < count - 1 else jnp.zeros_like(left[n])
                from_left = jnp.where(spot == 0, before, left[n])
                from_right = jnp.where(spot == 7, after, right[n])
                if n == 2:
                    from_left = jnp.where(spot == M, 0.0, from_left)
                    from_right = jnp.where(spot == M - 1, 0.0, from_right)
                mixed.append(sums[1][n] + from_left + from_right)
            centre = jnp.concatenate([mixed[0][:, None], mixed[1][:, None]], axis=1).reshape(4 * TW, 128)
            normed[pl.ds(pl.multiple_of(i * 4 * TW, 4 * TW), 4 * TW), lanes] = centre.astype(BF16)
            if side:
                normed[pl.ds(pl.multiple_of(middle + i * 32, 32), 32), lanes] = (
                    mixed[2].reshape(32, 128).astype(BF16)
                )
        return carry

    lax.fori_loop(0, rows // 4, convolve, 0)
    last[1].wait()


def halves(value):
    return jnp.concatenate([value[:, : D // 2], value[:, D // 2 :]], axis=0)


def tile_kernel(
    above, own, below, left, right, sides, strips, wq, wk, wv, wo, taps, wp,
    to_left, to_right, x_ref, normed, wp_s, centre, rims, out_side, part_sems, sems, *buffers,
):
    buffers = (*buffers[:4], wp_s, normed, *buffers[4:])
    copies, start = [], 0
    for i, piece in enumerate((above, own, below)):
        size = piece.shape[0]
        copies.append(pltpu.make_async_copy(piece, centre.at[pl.ds(start, size)], part_sems.at[i]))
        start += size
    copies.append(pltpu.make_async_copy(left, rims.at[pl.ds(0, STRIP)], part_sems.at[3]))
    copies.append(pltpu.make_async_copy(right, rims.at[pl.ds(STRIP, STRIP)], part_sems.at[4]))
    for copy in copies:
        copy.start()
    weights = (wq, wk, wv, wo, taps, wp)
    start_block(weights, buffers, sems, 0)
    group_matrices(buffers[-4], buffers[-3])
    sums = buffers[-2]
    sums[...] = jnp.zeros_like(sums)
    for copy in copies:
        copy.wait()
    for j in range(BLOCKS):
        block = slice(j * LANES, j * LANES + LANES)
        value = centre[:, block].astype(F32)
        x_ref[:SENT, block] = value
        add_sums(sums, block, value)
        value = dot(sides[...], rims[:, block])
        x_ref[SENT:, block] = value
        add_sums(sums, block, value)

    refine(WH, True, x_ref, weights, buffers, sems)
    for j in range(BLOCKS):
        block = slice(j * LANES, j * LANES + LANES)
        value = x_ref[SENT:, block] + dot(normed[SENT:, :], wp_s[:, block])
        out_side[:, block] = value.astype(BF16).astype(F32)
    for a in range(N_ROW):
        first = (a + M) % N_ROW
        lines = [out_side[(8 * k + first) * 8 : (8 * k + first + 1) * 8, :] for k in range(4)]
        rim = dot(strips[...], halves(jnp.concatenate(lines, axis=0).astype(BF16))).astype(BF16)
        to_right[a * 32 : a * 32 + 32, :] = rim[:32]
        to_left[a * 32 : a * 32 + 32, :] = rim[32:]


def rest_kernel(hidden, mixed, wp, mains, main, out):
    for j in range(BLOCKS):
        block = slice(j * LANES, j * LANES + LANES)
        out[:, block] = (hidden[:SENT, block] + dot(mixed[:SENT, :], wp[:, block])).astype(BF16)
    for a in range(N_ROW):
        first = (a + M) % N_ROW
        lines = [out[(8 * k + first) * TW : (8 * k + first + 1) * TW, :] for k in range(4)]
        main[a * 128 : a * 128 + 128, :] = dot(
            mains[...], halves(jnp.concatenate(lines, axis=0))
        ).astype(BF16)


def join_kernel(main, from_left, from_right, out):
    for a in range(N_ROW):
        first, last = a * 128, a * 128 + 96
        rim = slice(a * 32, a * 32 + 32)
        out[first : first + 32, :] = (
            main[first : first + 32, :].astype(F32) + from_left[rim, :].astype(F32)
        ).astype(BF16)
        out[first + 32 : last, :] = main[first + 32 : last, :]
        out[last : last + 32, :] = (
            main[last : last + 32, :].astype(F32) + from_right[rim, :].astype(F32)
        ).astype(BF16)


def sub_kernel(
    place, got, gathers, packing, wq, wk, wv, wo, taps, wp,
    result, gather, local, x_ref, out, gather_sem, sems, *buffers,
):
    weights = (wq, wk, wv, wo, taps, wp)
    copy = pltpu.make_async_copy(gathers.at[place[0]], gather, gather_sem)
    copy.start()
    start_block(weights, buffers, sems, 0)
    group_matrices(buffers[-4], buffers[-3])
    sums = buffers[-2]
    sums[...] = jnp.zeros_like(sums)
    late = place[1]
    copy.wait()
    for r in range(N_ROW):
        other = jnp.clip(r + 2 * late - 1, 0, N_ROW - 1)
        edge = 1 - late if r == 0 else late if r == N_ROW - 1 else 0
        cells = jnp.concatenate(
            [got[r * 128 : r * 128 + 128, :], got[pl.ds(pl.multiple_of(other * 128, 128), 128), :]],
            axis=0,
        )
        value = dot(gather[edge], cells).astype(BF16)
        at = slice(r * 48, r * 48 + 48)
        for h in range(2):
            half = slice(h * D // 2, h * D // 2 + D // 2)
            local[at, half] = value[h * 48 : h * 48 + 48]
            wide = value[h * 48 : h * 48 + 48].astype(F32)
            x_ref[at, half] = wide
            add_sums(sums, half, wide)

    refine(TH, False, x_ref, weights, buffers, sems)
    wp_s, normed = buffers[4:6]
    for j in range(BLOCKS):
        block = slice(j * LANES, j * LANES + LANES)
        value = x_ref[:, block] + dot(normed[...], wp_s[:, block])
        dilated = value.astype(BF16).astype(F32)
        out[:, block] = (0.6 * local[:, block].astype(F32) + 0.4 * dilated).astype(BF16)
    for r in range(N_ROW):
        at = slice(r * 48, r * 48 + 48)
        cells = jnp.concatenate([out[at, t * LANES : t * LANES + LANES] for t in range(BLOCKS)], axis=0)
        packed = dot(packing[...], cells).astype(BF16)
        result[r * 128 : r * 128 + 128, :LANES] = packed[:128]
        result[r * 128 : r * 128 + 128, LANES:] = packed[128:]


def unpack_kernel(got, packing, out):
    for a in range(N_ROW):
        at = slice(a * 128, a * 128 + 128)
        cells = jnp.concatenate([got[at, :LANES], got[at, LANES:]], axis=0)
        value = lax.dot_general(
            packing[...], cells, (((0,), (0,)), ((), ())), preferred_element_type=F32
        ).astype(BF16)
        for t in range(BLOCKS):
            for i in range(PART_H):
                to = (i * N_ROW + a) * TW
                out[to : to + TW, t * LANES : t * LANES + LANES] = value[
                    t * 48 + i * TW : t * 48 + i * TW + TW
                ]


def scratch(cells, padded):
    heads = pltpu.VMEM((BLOCKS, cells, LANES), BF16)
    blocks = pltpu.VMEM((BLOCKS, D, LANES), BF16)
    square = pltpu.VMEM((D, D), BF16)
    return [
        pltpu.SemaphoreType.DMA((5, BLOCKS)),
        blocks, blocks, blocks, square, square,
        pltpu.VMEM((cells, D), BF16),
        heads, heads, heads,
        pltpu.VMEM((cells, D), BF16),
        pltpu.VMEM((padded, D), F32),
        pltpu.VMEM((2, 8, 128), F32),
        pltpu.VMEM((D, 128), BF16),
        pltpu.VMEM((128, D), BF16),
        pltpu.VMEM((16, D), F32),
        pltpu.VMEM((8, D), F32),
    ]


ANY = pl.BlockSpec(memory_space=pl.ANY)
HBM = pl.BlockSpec(memory_space=pltpu.HBM)
VMEM = pl.BlockSpec(memory_space=pltpu.VMEM)


def params(mib):
    return pltpu.CompilerParams(vmem_limit_bytes=mib * 2**20)


def tile_block(above, own, below, left, right, weights):
    shape = jax.ShapeDtypeStruct
    sems, *buffers = scratch(WIN, (WH + 2) * WW)
    to_left, to_right, hidden, mixed, w_proj = pl.pallas_call(
        tile_kernel,
        out_shape=(
            shape((2 * STRIP, D // 2), BF16),
            shape((2 * STRIP, D // 2), BF16),
            shape((WIN, D), F32),
            shape((WIN, D), BF16),
            shape((D, D), BF16),
        ),
        in_specs=[ANY] * 5 + [VMEM] * 2 + [HBM] * 4 + [VMEM, HBM],
        out_specs=(VMEM,) * 5,
        scratch_shapes=[
            pltpu.VMEM((SENT, D), BF16),
            pltpu.VMEM((SIDE, D), BF16),
            pltpu.VMEM((SIDE, D), F32),
            pltpu.SemaphoreType.DMA((5,)),
            sems,
            *buffers[:4],
            *buffers[6:],
        ],
        compiler_params=params(TILE_MIB),
        name="tile_block",
    )(above, own, below, left, right, side_matrix(), strip_matrix(), *weights)
    main = pl.pallas_call(
        rest_kernel,
        out_shape=shape((2 * SENT, D // 2), BF16),
        in_specs=[VMEM] * 4,
        out_specs=VMEM,
        scratch_shapes=[pltpu.VMEM((SENT, D), BF16)],
        compiler_params=params(REST_MIB),
        name="rest",
    )(hidden, mixed, w_proj, main_matrix())
    return main, to_left, to_right


def join(main, from_left, from_right):
    return pl.pallas_call(
        join_kernel,
        out_shape=jax.ShapeDtypeStruct(main.shape, BF16),
        in_specs=[VMEM] * 3,
        out_specs=VMEM,
        compiler_params=params(8),
        name="join",
    )(main, from_left, from_right)


def sub_block(place, got, weights):
    return pl.pallas_call(
        sub_kernel,
        out_shape=jax.ShapeDtypeStruct((DEV * 8, 2 * LANES), BF16),
        in_specs=[pl.BlockSpec(memory_space=pltpu.SMEM), VMEM, HBM, VMEM] + [HBM] * 4 + [VMEM, HBM],
        out_specs=VMEM,
        scratch_shapes=[
            pltpu.VMEM((2, 96, 256), BF16),
            pltpu.VMEM((OWN, D), BF16),
            pltpu.VMEM((OWN, D), F32),
            pltpu.VMEM((OWN, D), BF16),
            pltpu.SemaphoreType.DMA,
            *scratch(OWN, (TH + 2) * TW),
        ],
        compiler_params=params(48),
        name="sub_block",
    )(place, got, gather_matrices(), packing_matrix(), *weights)


def unpack(got):
    return pl.pallas_call(
        unpack_kernel,
        out_shape=jax.ShapeDtypeStruct((OWN, D), BF16),
        in_specs=[VMEM] * 2,
        out_specs=VMEM,
        compiler_params=params(8),
        name="unpack",
    )(got, packing_matrix())


def shift(value, axis, step):
    count = lax.axis_size(axis)
    pairs = [(i, i + step) for i in range(count) if 0 <= i + step < count]
    return lax.ppermute(value, axis, pairs)


def body(latent, w_query, w_key, w_value, w_out, depth_kernel, w_proj):
    weights = (w_query, w_key, w_value, w_out, depth_kernel, w_proj)
    row, col = lax.axis_index("row"), lax.axis_index("col")
    late = (row >= M).astype(jnp.int32)
    kind = (col >= M).astype(jnp.int32) + (col >= TW - M).astype(jnp.int32)
    place = jnp.stack([3 * late + kind, late])
    above = shift(latent[TH - M :], "row", 1)
    below = shift(latent[:M], "row", -1)
    tall = jnp.concatenate([above, latent, below], axis=0)
    left = shift(tall[:, TW - M :].reshape(STRIP, D), "col", 1)
    right = shift(tall[:, :M].reshape(STRIP, D), "col", -1)
    main, to_left, to_right = tile_block(
        above.reshape(M * TW, D), latent.reshape(OWN, D), below.reshape(M * TW, D),
        left, right, weights,
    )
    main = join(main, shift(to_right, "col", 1), shift(to_left, "col", -1))
    both = functools.partial(
        lax.all_to_all, axis_name=("row", "col"), split_axis=0, concat_axis=0, tiled=True
    )
    got = both(main.reshape(DEV, 8, D // 2)).reshape(2 * SENT, D // 2)
    refined = sub_block(place, got, weights)
    back = both(refined.reshape(DEV, 8, 2 * LANES)).reshape(DEV * 8, 2 * LANES)
    return unpack(back).reshape(TH, TW, D)


def solution(mesh):
    return jax.shard_map(
        body,
        mesh=mesh,
        in_specs=(P("row", "col", None), P(), P(), P(), P(), P(), P()),
        out_specs=P("row", "col", None),
        check_vma=False,
    )
```

```python
import functools

import jax
import jax.numpy as jnp
import numpy as np
from jax import lax
from jax.experimental import pallas as pl
from jax.experimental.pallas import tpu as pltpu
from jax.sharding import PartitionSpec as P

D = 1280
HEADS = 20
HEAD = D // HEADS
GROUPS = 32
GROUP = D // GROUPS
M = 4
TH = 24
TW = 16
WH = TH + 2 * M
WW = TW + 2 * M
OWN = TH * TW
WIN = WH * WW
N_ROW = 8
N_COL = 16
DEV = N_ROW * N_COL
SENT = WH * TW
STRIP = WH * M
SIDE = 2 * STRIP
PART_H = TH // N_ROW
LANES = 256
BLOCKS = D // LANES
F32 = jnp.float32
BF16 = jnp.bfloat16
HIGH_SUM = 2.0**100
LOW_SUM = 2.0**-100
TILE_MIB = 46
REST_MIB = 14


def side_matrix():
    out = np.zeros((SIDE, SIDE), np.float32)
    for w in range(WH):
        for c in range(M):
            out[w * 8 + c, STRIP + w * M + c] = 1
            out[w * 8 + M + c, w * M + c] = 1
    return out.astype(jnp.bfloat16)


def main_matrix():
    out = np.zeros((128, 128), np.float32)
    for b in range(TW):
        for h in range(2):
            for k in range(4):
                out[b * 8 + h * 4 + k, h * 64 + k * TW + b] = 1
    return out.astype(jnp.bfloat16)


def strip_matrix():
    out = np.zeros((64, 64), np.float32)
    for b in range(M):
        for h in range(2):
            for k in range(4):
                out[b * 8 + h * 4 + k, h * 32 + k * 8 + b] = 1
                out[32 + b * 8 + h * 4 + k, h * 32 + k * 8 + M + b] = 1
    return out.astype(jnp.bfloat16)


def gather_matrices():
    out = np.zeros((2, 3, 2, 96, 256), np.float32)
    for late in range(2):
        for kind in range(3):
            for edge in range(2):
                for h in range(2):
                    for i in range(PART_H):
                        for c in range(N_COL):
                            two_cols = (kind == 0 and c > 0) or (kind == 2 and c < N_COL - 1)
                            shared = i == (2 if late else 0) and not edge
                            scale = (0.5 if two_cols else 1.0) * (0.5 if shared else 1.0)
                            to = h * 48 + i * TW + c
                            out[late, kind, edge, to, c * 8 + h * 4 + i + late] = scale
                            if shared:
                                out[late, kind, edge, to, 128 + c * 8 + h * 4 + (0 if late else 3)] = scale
    return out.reshape(6, 2, 96, 256).astype(jnp.bfloat16)


def packing_matrix():
    out = np.zeros((256, 240), np.float32)
    for t in range(5):
        for i in range(PART_H):
            for c in range(N_COL):
                at = 10 * i + 2 * t
                out[(at % 4) // 2 * 128 + c * 8 + at // 4, t * 48 + i * TW + c] = 1
    return out.astype(jnp.bfloat16)


def dot(a, b):
    return jnp.dot(a, b, preferred_element_type=F32)


def six_parts(first, second):
    shape = (8, first.shape[1])
    which = lax.broadcasted_iota(jnp.int32, shape, 0)
    full = jnp.where(which < 3, jnp.broadcast_to(first, shape), jnp.broadcast_to(second, shape))
    high = full.astype(BF16).astype(F32)
    rest = full - high
    mid = rest.astype(BF16).astype(F32)
    low = rest - mid
    part = jnp.where(which < 3, which, which - 3)
    parts = jnp.where(part == 0, high, jnp.where(part == 1, mid, low))
    return jnp.where(which < 6, parts, 0.0).astype(BF16)


def two_rows(parts):
    return parts[0:1] + parts[1:2] + parts[2:3], parts[3:4] + parts[4:5] + parts[5:6]


def group_matrices(member, spread):
    for ref, chan_axis in ((member, 0), (spread, 1)):
        chan = lax.broadcasted_iota(jnp.int32, ref.shape, chan_axis)
        first = GROUP * lax.broadcasted_iota(jnp.int32, ref.shape, 1 - chan_axis)
        inside = jnp.logical_and(chan >= first, chan < first + GROUP)
        ref[...] = jnp.where(inside, 1.0, 0.0).astype(BF16)


def add_sums(sums, lanes, value):
    tiles = value.reshape(value.shape[0] // 8, 8, value.shape[1])
    sums[0:8, lanes] += jnp.sum(tiles, axis=0)
    sums[8:16, lanes] += jnp.sum(tiles * tiles, axis=0)


def group_stats(x_ref, sums, stats, member, spread):
    scale = 1.0 / (GROUP * x_ref.shape[0])

    def means(first, second):
        first, second = two_rows(dot(six_parts(first, second), member[...]))
        return first * scale, second * scale

    def spread_out(mean, var):
        rstd = 1.0 / jnp.sqrt(jnp.maximum(var, 0.0) + 1e-05)
        mean, rstd = two_rows(dot(six_parts(mean, rstd), spread[...]))
        stats[0:1] = mean
        stats[1:2] = rstd

    total = jnp.sum(sums[0:8], axis=0, keepdims=True)
    mean, square = means(total, jnp.sum(sums[8:16], axis=0, keepdims=True))
    var = square - mean * mean
    spread_out(mean, var)

    @pl.when(jnp.logical_not(jnp.min(var - 0.01 * mean * mean) >= 0.0))
    def _():
        centred = jnp.square(x_ref[...] - stats[0:1])
        _, var = means(total, jnp.sum(centred, axis=0, keepdims=True))
        spread_out(mean, var)

    return stats[0:1], stats[1:2]


def safe_head(j, pair, half, q_ref, k_ref, v_ref):
    lanes = pl.ds(pair * 128, 128)
    query = q_ref[j, :, lanes]
    lane = lax.broadcasted_iota(jnp.int32, query.shape, 1)
    query = jnp.where((lane // HEAD) == half, query.astype(F32), 0.0).astype(BF16)
    scores = lax.dot_general(
        query, k_ref[j, :, lanes], (((1,), (1,)), ((), ())), preferred_element_type=F32
    )
    expo = jnp.exp(scores - jnp.max(scores, axis=1, keepdims=True))
    probs = (expo / jnp.sum(expo, axis=1, keepdims=True)).astype(BF16)
    return dot(probs, v_ref[j, :, lanes])


def weight_copies(weights, buffers, sems):
    wq, wk, wv, wo, _, wp = weights

    def block(i, j):
        src = (wq, wk, wv)[i]
        return pltpu.make_async_copy(
            src.at[:, pl.ds(pl.multiple_of(j * LANES, LANES), LANES)], buffers[i].at[j], sems.at[i, j]
        )

    last = [
        pltpu.make_async_copy(wo, buffers[3], sems.at[3, 0]),
        pltpu.make_async_copy(wp, buffers[4], sems.at[4, 0]),
    ]
    return block, last


def start_block(weights, buffers, sems, j):
    block, _ = weight_copies(weights, buffers, sems)
    for i in range(3):
        block(i, j).start()


def refine(rows, side, x_ref, weights, buffers, sems):
    cells = x_ref.shape[0]
    middle = rows * TW
    taps = weights[4]
    wq_s, wk_s, wv_s, wo_s, wp_s, normed, q_ref, k_ref, v_ref, att, act, range_ref, member, spread, sums, stats = buffers
    weight_block, last = weight_copies(weights, buffers, sems)

    start_block(weights, buffers, sems, 1)
    mean, rstd = group_stats(x_ref, sums, stats, member, spread)
    normed[...] = ((x_ref[...] - mean) * rstd).astype(BF16)
    range_ref[0] = jnp.full((8, 128), 1.0, F32)
    range_ref[1] = jnp.full((8, 128), 1.0, F32)

    def heads(j, carry):
        @pl.when(j < BLOCKS - 2)
        def _():
            start_block(weights, buffers, sems, j + 2)

        @pl.when(j == BLOCKS - 2)
        def _():
            last[0].start()

        @pl.when(j == BLOCKS - 1)
        def _():
            last[1].start()

        for i in range(3):
            weight_block(i, j).wait()
        n = normed[...]
        q_ref[j] = (dot(n, wq_s[j]) * (1.0 / 8.0)).astype(BF16)
        k_ref[j] = dot(n, wk_s[j]).astype(BF16)
        v_ref[j] = dot(n, wv_s[j]).astype(BF16)
        lane = lax.broadcasted_iota(jnp.int32, (cells, 128), 1)
        low, high = range_ref[0], range_ref[1]
        for pair in range(2):
            lanes = slice(pair * 128, pair * 128 + 128)
            query = q_ref[j, :, lanes]
            key = k_ref[j, :, lanes]
            value = jnp.concatenate([v_ref[j, :, lanes], jnp.ones((cells, 128), BF16)], axis=1)
            done = []
            for half in range(2):
                mine = jnp.where((lane < HEAD) == (half == 0), query, jnp.zeros_like(query))
                scores = lax.dot_general(
                    mine, key, (((1,), (1,)), ((), ())), preferred_element_type=F32
                )
                out = dot(jnp.exp(scores).astype(BF16), value)
                total = out[:, 128:]
                low = jnp.minimum(low, jnp.min(total.reshape(cells // 8, 8, 128), axis=0))
                high = jnp.maximum(high, jnp.max(total.reshape(cells // 8, 8, 128), axis=0))
                done.append(out[:, :128] / total)
            att[:, pl.ds(pl.multiple_of(j * LANES + pair * 128, 128), 128)] = jnp.where(
                lane < HEAD, done[0], done[1]
            ).astype(BF16)
        range_ref[0] = low
        range_ref[1] = high
        return carry

    lax.fori_loop(0, BLOCKS, heads, 0)
    in_range = jnp.logical_and(jnp.min(range_ref[0]) > LOW_SUM, jnp.max(range_ref[1]) < HIGH_SUM)

    @pl.when(jnp.logical_not(in_range))
    def _():
        def again(j, carry):
            lane = lax.broadcasted_iota(jnp.int32, (cells, 128), 1)
            for pair in range(2):
                done = [safe_head(j, pair, half, q_ref, k_ref, v_ref) for half in range(2)]
                att[:, pl.ds(pl.multiple_of(j * LANES + pair * 128, 128), 128)] = jnp.where(
                    lane < HEAD, done[0], done[1]
                ).astype(BF16)
            return carry

        lax.fori_loop(0, BLOCKS, again, 0)

    sums[...] = jnp.zeros_like(sums)
    last[0].wait()
    for j in range(BLOCKS):
        block = slice(j * LANES, j * LANES + LANES)
        hidden = x_ref[:, block] + dot(att[...], wo_s[:, block])
        x_ref[:, block] = hidden
        add_sums(sums, block, hidden)

    mean, rstd = group_stats(x_ref, sums, stats, member, spread)
    second = (rows + 2) * TW
    for start, width in ((0, TW), (second, 8)) if side else ((0, TW),):
        act[pl.ds(start, width), :] = jnp.zeros((width, D), F32)
        act[pl.ds(start + (rows + 1) * width, width), :] = jnp.zeros((width, D), F32)
    half_rstd = 0.5 * rstd
    parts = ((0, 0, TW), (middle, second, 8)) if side else ((0, 0, TW),)

    def activate(i, carry):
        for start, place, width in parts:
            size = 4 * width
            at = pl.ds(pl.multiple_of(start + i * size, size), size)
            half = (x_ref[at, :] - mean) * half_rstd
            to = pl.ds(pl.multiple_of(place + width + i * size, 8), size)
            act[to, :] = half + half * jnp.tanh(half)
        return carry

    lax.fori_loop(0, rows // 4, activate, 0)

    def convolve(i, carry):
        spot = lax.broadcasted_iota(jnp.int32, (4, 8, 128), 1)
        for t in range(D // 128):
            lanes = slice(t * 128, t * 128 + 128)
            weight = [taps[n : n + 1, lanes] for n in range(9)]
            sums = [[], [], []]
            for start, place, width in parts:
                size = 4 * width
                lines = [
                    act[pl.ds(pl.multiple_of(place + i * size + d * width, 8), size), lanes]
                    for d in range(3)
                ]
                for dj in range(3):
                    part = lines[0] * weight[dj] + lines[1] * weight[3 + dj] + lines[2] * weight[6 + dj]
                    part = part.reshape(4, width // 8, 8, 128)
                    sums[dj] += [part[:, n] for n in range(width // 8)]
            left = [pltpu.roll(v, 1, 1) for v in sums[0]]
            right = [pltpu.roll(v, 7, 1) for v in sums[2]]
            count = len(left)
            mixed = []
            for n in range(count):
                before = left[n - 1] if side or n > 0 else jnp.zeros_like(left[n])
                after = right[(n + 1) % count] if side or n < count - 1 else jnp.zeros_like(left[n])
                from_left = jnp.where(spot == 0, before, left[n])
                from_right = jnp.where(spot == 7, after, right[n])
                if n == 2:
                    from_left = jnp.where(spot == M, 0.0, from_left)
                    from_right = jnp.where(spot == M - 1, 0.0, from_right)
                mixed.append(sums[1][n] + from_left + from_right)
            centre = jnp.concatenate([mixed[0][:, None], mixed[1][:, None]], axis=1).reshape(4 * TW, 128)
            normed[pl.ds(pl.multiple_of(i * 4 * TW, 4 * TW), 4 * TW), lanes] = centre.astype(BF16)
            if side:
                normed[pl.ds(pl.multiple_of(middle + i * 32, 32), 32), lanes] = (
                    mixed[2].reshape(32, 128).astype(BF16)
                )
        return carry

    lax.fori_loop(0, rows // 4, convolve, 0)
    last[1].wait()


def halves(value):
    return jnp.concatenate([value[:, : D // 2], value[:, D // 2 :]], axis=0)


def tile_kernel(
    above, own, below, left, right, sides, strips, wq, wk, wv, wo, taps, wp,
    to_left, to_right, x_ref, normed, wp_s, centre, rims, out_side, part_sems, sems, *buffers,
):
    buffers = (*buffers[:4], wp_s, normed, *buffers[4:])
    copies, start = [], 0
    for i, piece in enumerate((above, own, below)):
        size = piece.shape[0]
        copies.append(pltpu.make_async_copy(piece, centre.at[pl.ds(start, size)], part_sems.at[i]))
        start += size
    copies.append(pltpu.make_async_copy(left, rims.at[pl.ds(0, STRIP)], part_sems.at[3]))
    copies.append(pltpu.make_async_copy(right, rims.at[pl.ds(STRIP, STRIP)], part_sems.at[4]))
    for copy in copies:
        copy.start()
    weights = (wq, wk, wv, wo, taps, wp)
    start_block(weights, buffers, sems, 0)
    group_matrices(buffers[-4], buffers[-3])
    sums = buffers[-2]
    sums[...] = jnp.zeros_like(sums)
    for copy in copies:
        copy.wait()
    for j in range(BLOCKS):
        block = slice(j * LANES, j * LANES + LANES)
        value = centre[:, block].astype(F32)
        x_ref[:SENT, block] = value
        add_sums(sums, block, value)
        value = dot(sides[...], rims[:, block])
        x_ref[SENT:, block] = value
        add_sums(sums, block, value)

    refine(WH, True, x_ref, weights, buffers, sems)
    for j in range(BLOCKS):
        block = slice(j * LANES, j * LANES + LANES)
        value = x_ref[SENT:, block] + dot(normed[SENT:, :], wp_s[:, block])
        out_side[:, block] = value.astype(BF16).astype(F32)
    for a in range(N_ROW):
        first = (a + M) % N_ROW
        lines = [out_side[(8 * k + first) * 8 : (8 * k + first + 1) * 8, :] for k in range(4)]
        rim = dot(strips[...], halves(jnp.concatenate(lines, axis=0).astype(BF16))).astype(BF16)
        to_right[a * 32 : a * 32 + 32, :] = rim[:32]
        to_left[a * 32 : a * 32 + 32, :] = rim[32:]


def rest_kernel(hidden, mixed, wp, mains, main, out):
    for j in range(BLOCKS):
        block = slice(j * LANES, j * LANES + LANES)
        out[:, block] = (hidden[:SENT, block] + dot(mixed[:SENT, :], wp[:, block])).astype(BF16)
    for a in range(N_ROW):
        first = (a + M) % N_ROW
        lines = [out[(8 * k + first) * TW : (8 * k + first + 1) * TW, :] for k in range(4)]
        main[a * 128 : a * 128 + 128, :] = dot(
            mains[...], halves(jnp.concatenate(lines, axis=0))
        ).astype(BF16)


def join_kernel(main, from_left, from_right, out):
    for a in range(N_ROW):
        first, last = a * 128, a * 128 + 96
        rim = slice(a * 32, a * 32 + 32)
        out[first : first + 32, :] = (
            main[first : first + 32, :].astype(F32) + from_left[rim, :].astype(F32)
        ).astype(BF16)
        out[first + 32 : last, :] = main[first + 32 : last, :]
        out[last : last + 32, :] = (
            main[last : last + 32, :].astype(F32) + from_right[rim, :].astype(F32)
        ).astype(BF16)


def sub_kernel(
    place, got, gathers, packing, wq, wk, wv, wo, taps, wp,
    result, gather, local, x_ref, out, gather_sem, sems, *buffers,
):
    weights = (wq, wk, wv, wo, taps, wp)
    copy = pltpu.make_async_copy(gathers.at[place[0]], gather, gather_sem)
    copy.start()
    start_block(weights, buffers, sems, 0)
    group_matrices(buffers[-4], buffers[-3])
    sums = buffers[-2]
    sums[...] = jnp.zeros_like(sums)
    late = place[1]
    copy.wait()
    for r in range(N_ROW):
        other = jnp.clip(r + 2 * late - 1, 0, N_ROW - 1)
        edge = 1 - late if r == 0 else late if r == N_ROW - 1 else 0
        cells = jnp.concatenate(
            [got[r * 128 : r * 128 + 128, :], got[pl.ds(pl.multiple_of(other * 128, 128), 128), :]],
            axis=0,
        )
        value = dot(gather[edge], cells).astype(BF16)
        at = slice(r * 48, r * 48 + 48)
        for h in range(2):
            half = slice(h * D // 2, h * D // 2 + D // 2)
            local[at, half] = value[h * 48 : h * 48 + 48]
            wide = value[h * 48 : h * 48 + 48].astype(F32)
            x_ref[at, half] = wide
            add_sums(sums, half, wide)

    refine(TH, False, x_ref, weights, buffers, sems)
    wp_s, normed = buffers[4:6]
    for j in range(BLOCKS):
        block = slice(j * LANES, j * LANES + LANES)
        value = x_ref[:, block] + dot(normed[...], wp_s[:, block])
        dilated = value.astype(BF16).astype(F32)
        out[:, block] = (0.6 * local[:, block].astype(F32) + 0.4 * dilated).astype(BF16)
    for r in range(N_ROW):
        at = slice(r * 48, r * 48 + 48)
        cells = jnp.concatenate([out[at, t * LANES : t * LANES + LANES] for t in range(BLOCKS)], axis=0)
        packed = dot(packing[...], cells).astype(BF16)
        result[r * 128 : r * 128 + 128, :LANES] = packed[:128]
        result[r * 128 : r * 128 + 128, LANES:] = packed[128:]


def unpack_kernel(got, packing, out):
    for a in range(N_ROW):
        at = slice(a * 128, a * 128 + 128)
        cells = jnp.concatenate([got[at, :LANES], got[at, LANES:]], axis=0)
        value = lax.dot_general(
            packing[...], cells, (((0,), (0,)), ((), ())), preferred_element_type=F32
        ).astype(BF16)
        for t in range(BLOCKS):
            for i in range(PART_H):
                to = (i * N_ROW + a) * TW
                out[to : to + TW, t * LANES : t * LANES + LANES] = value[
                    t * 48 + i * TW : t * 48 + i * TW + TW
                ]


def scratch(cells, padded):
    heads = pltpu.VMEM((BLOCKS, cells, LANES), BF16)
    blocks = pltpu.VMEM((BLOCKS, D, LANES), BF16)
    square = pltpu.VMEM((D, D), BF16)
    return [
        pltpu.SemaphoreType.DMA((5, BLOCKS)),
        blocks, blocks, blocks, square, square,
        pltpu.VMEM((cells, D), BF16),
        heads, heads, heads,
        pltpu.VMEM((cells, D), BF16),
        pltpu.VMEM((padded, D), F32),
        pltpu.VMEM((2, 8, 128), F32),
        pltpu.VMEM((D, 128), BF16),
        pltpu.VMEM((128, D), BF16),
        pltpu.VMEM((16, D), F32),
        pltpu.VMEM((8, D), F32),
    ]


ANY = pl.BlockSpec(memory_space=pl.ANY)
HBM = pl.BlockSpec(memory_space=pltpu.HBM)
VMEM = pl.BlockSpec(memory_space=pltpu.VMEM)


def params(mib):
    return pltpu.CompilerParams(vmem_limit_bytes=mib * 2**20)


def tile_block(above, own, below, left, right, weights):
    shape = jax.ShapeDtypeStruct
    sems, *buffers = scratch(WIN, (WH + 2) * WW)
    to_left, to_right, hidden, mixed, w_proj = pl.pallas_call(
        tile_kernel,
        out_shape=(
            shape((2 * STRIP, D // 2), BF16),
            shape((2 * STRIP, D // 2), BF16),
            shape((WIN, D), F32),
            shape((WIN, D), BF16),
            shape((D, D), BF16),
        ),
        in_specs=[ANY] * 5 + [VMEM] * 2 + [HBM] * 4 + [VMEM, HBM],
        out_specs=(VMEM,) * 5,
        scratch_shapes=[
            pltpu.VMEM((SENT, D), BF16),
            pltpu.VMEM((SIDE, D), BF16),
            pltpu.VMEM((SIDE, D), F32),
            pltpu.SemaphoreType.DMA((5,)),
            sems,
            *buffers[:4],
            *buffers[6:],
        ],
        compiler_params=params(TILE_MIB),
        name="tile_block",
    )(above, own, below, left, right, side_matrix(), strip_matrix(), *weights)
    main = pl.pallas_call(
        rest_kernel,
        out_shape=shape((2 * SENT, D // 2), BF16),
        in_specs=[VMEM] * 4,
        out_specs=VMEM,
        scratch_shapes=[pltpu.VMEM((SENT, D), BF16)],
        compiler_params=params(REST_MIB),
        name="rest",
    )(hidden, mixed, w_proj, main_matrix())
    return main, to_left, to_right


def join(main, from_left, from_right):
    return pl.pallas_call(
        join_kernel,
        out_shape=jax.ShapeDtypeStruct(main.shape, BF16),
        in_specs=[VMEM] * 3,
        out_specs=VMEM,
        compiler_params=params(8),
        name="join",
    )(main, from_left, from_right)


def sub_block(place, got, weights):
    return pl.pallas_call(
        sub_kernel,
        out_shape=jax.ShapeDtypeStruct((DEV * 8, 2 * LANES), BF16),
        in_specs=[pl.BlockSpec(memory_space=pltpu.SMEM), VMEM, HBM, VMEM] + [HBM] * 4 + [VMEM, HBM],
        out_specs=VMEM,
        scratch_shapes=[
            pltpu.VMEM((2, 96, 256), BF16),
            pltpu.VMEM((OWN, D), BF16),
            pltpu.VMEM((OWN, D), F32),
            pltpu.VMEM((OWN, D), BF16),
            pltpu.SemaphoreType.DMA,
            *scratch(OWN, (TH + 2) * TW),
        ],
        compiler_params=params(48),
        name="sub_block",
    )(place, got, gather_matrices(), packing_matrix(), *weights)


def unpack(got):
    return pl.pallas_call(
        unpack_kernel,
        out_shape=jax.ShapeDtypeStruct((OWN, D), BF16),
        in_specs=[VMEM] * 2,
        out_specs=VMEM,
        compiler_params=params(8),
        name="unpack",
    )(got, packing_matrix())


def shift(value, axis, step):
    count = lax.axis_size(axis)
    pairs = [(i, i + step) for i in range(count) if 0 <= i + step < count]
    return lax.ppermute(value, axis, pairs)


def body(latent, w_query, w_key, w_value, w_out, depth_kernel, w_proj):
    weights = (w_query, w_key, w_value, w_out, depth_kernel, w_proj)
    row, col = lax.axis_index("row"), lax.axis_index("col")
    late = (row >= M).astype(jnp.int32)
    kind = (col >= M).astype(jnp.int32) + (col >= TW - M).astype(jnp.int32)
    place = jnp.stack([3 * late + kind, late])
    above = shift(latent[TH - M :], "row", 1)
    below = shift(latent[:M], "row", -1)
    tall = jnp.concatenate([above, latent, below], axis=0)
    left = shift(tall[:, TW - M :].reshape(STRIP, D), "col", 1)
    right = shift(tall[:, :M].reshape(STRIP, D), "col", -1)
    main, to_left, to_right = tile_block(
        above.reshape(M * TW, D), latent.reshape(OWN, D), below.reshape(M * TW, D),
        left, right, weights,
    )
    main = join(main, shift(to_right, "col", 1), shift(to_left, "col", -1))
    both = functools.partial(
        lax.all_to_all, axis_name=("row", "col"), split_axis=0, concat_axis=0, tiled=True
    )
    got = both(main.reshape(DEV, 8, D // 2)).reshape(2 * SENT, D // 2)
    refined = sub_block(place, got, weights)
    back = both(refined.reshape(DEV, 8, 2 * LANES)).reshape(DEV * 8, 2 * LANES)
    return unpack(back).reshape(TH, TW, D)


def solution(mesh):
    return jax.shard_map(
        body,
        mesh=mesh,
        in_specs=(P("row", "col", None), P(), P(), P(), P(), P(), P()),
        out_specs=P("row", "col", None),
        check_vma=False,
    )
```

```python
import functools

import jax
import jax.numpy as jnp
import numpy as np
from jax import lax
from jax.experimental import pallas as pl
from jax.experimental.pallas import tpu as pltpu
from jax.sharding import PartitionSpec as P

D = 1280
HEADS = 20
HEAD = D // HEADS
GROUPS = 32
GROUP = D // GROUPS
M = 4
TH = 24
TW = 16
WH = TH + 2 * M
WW = TW + 2 * M
OWN = TH * TW
WIN = WH * WW
N_ROW = 8
N_COL = 16
DEV = N_ROW * N_COL
SENT = WH * TW
STRIP = WH * M
SIDE = 2 * STRIP
PART_H = TH // N_ROW
LANES = 256
BLOCKS = D // LANES
F32 = jnp.float32
BF16 = jnp.bfloat16
HIGH_SUM = 2.0**100
LOW_SUM = 2.0**-100
TILE_MIB = 46
REST_MIB = 14


def side_matrix():
    out = np.zeros((SIDE, SIDE), np.float32)
    for w in range(WH):
        for c in range(M):
            out[w * 8 + c, STRIP + w * M + c] = 1
            out[w * 8 + M + c, w * M + c] = 1
    return out.astype(jnp.bfloat16)


def main_matrix():
    out = np.zeros((128, 128), np.float32)
    for b in range(TW):
        for h in range(2):
            for k in range(4):
                out[b * 8 + h * 4 + k, h * 64 + k * TW + b] = 1
    return out.astype(jnp.bfloat16)


def strip_matrix():
    out = np.zeros((64, 64), np.float32)
    for b in range(M):
        for h in range(2):
            for k in range(4):
                out[b * 8 + h * 4 + k, h * 32 + k * 8 + b] = 1
                out[32 + b * 8 + h * 4 + k, h * 32 + k * 8 + M + b] = 1
    return out.astype(jnp.bfloat16)


def gather_matrices():
    out = np.zeros((2, 3, 2, 96, 256), np.float32)
    for late in range(2):
        for kind in range(3):
            for edge in range(2):
                for h in range(2):
                    for i in range(PART_H):
                        for c in range(N_COL):
                            two_cols = (kind == 0 and c > 0) or (kind == 2 and c < N_COL - 1)
                            shared = i == (2 if late else 0) and not edge
                            scale = (0.5 if two_cols else 1.0) * (0.5 if shared else 1.0)
                            to = h * 48 + i * TW + c
                            out[late, kind, edge, to, c * 8 + h * 4 + i + late] = scale
                            if shared:
                                out[late, kind, edge, to, 128 + c * 8 + h * 4 + (0 if late else 3)] = scale
    return out.reshape(6, 2, 96, 256).astype(jnp.bfloat16)


def packing_matrix():
    out = np.zeros((256, 240), np.float32)
    for t in range(5):
        for i in range(PART_H):
            for c in range(N_COL):
                at = 10 * i + 2 * t
                out[(at % 4) // 2 * 128 + c * 8 + at // 4, t * 48 + i * TW + c] = 1
    return out.astype(jnp.bfloat16)


def dot(a, b):
    return jnp.dot(a, b, preferred_element_type=F32)


def six_parts(first, second):
    shape = (8, first.shape[1])
    which = lax.broadcasted_iota(jnp.int32, shape, 0)
    full = jnp.where(which < 3, jnp.broadcast_to(first, shape), jnp.broadcast_to(second, shape))
    high = full.astype(BF16).astype(F32)
    rest = full - high
    mid = rest.astype(BF16).astype(F32)
    low = rest - mid
    part = jnp.where(which < 3, which, which - 3)
    parts = jnp.where(part == 0, high, jnp.where(part == 1, mid, low))
    return jnp.where(which < 6, parts, 0.0).astype(BF16)


def two_rows(parts):
    return parts[0:1] + parts[1:2] + parts[2:3], parts[3:4] + parts[4:5] + parts[5:6]


def group_matrices(member, spread):
    for ref, chan_axis in ((member, 0), (spread, 1)):
        chan = lax.broadcasted_iota(jnp.int32, ref.shape, chan_axis)
        first = GROUP * lax.broadcasted_iota(jnp.int32, ref.shape, 1 - chan_axis)
        inside = jnp.logical_and(chan >= first, chan < first + GROUP)
        ref[...] = jnp.where(inside, 1.0, 0.0).astype(BF16)


def add_sums(sums, lanes, value):
    tiles = value.reshape(value.shape[0] // 8, 8, value.shape[1])
    sums[0:8, lanes] += jnp.sum(tiles, axis=0)
    sums[8:16, lanes] += jnp.sum(tiles * tiles, axis=0)


def group_stats(x_ref, sums, stats, member, spread):
    scale = 1.0 / (GROUP * x_ref.shape[0])

    def means(first, second):
        first, second = two_rows(dot(six_parts(first, second), member[...]))
        return first * scale, second * scale

    def spread_out(mean, var):
        rstd = 1.0 / jnp.sqrt(jnp.maximum(var, 0.0) + 1e-05)
        mean, rstd = two_rows(dot(six_parts(mean, rstd), spread[...]))
        stats[0:1] = mean
        stats[1:2] = rstd

    total = jnp.sum(sums[0:8], axis=0, keepdims=True)
    mean, square = means(total, jnp.sum(sums[8:16], axis=0, keepdims=True))
    var = square - mean * mean
    spread_out(mean, var)

    @pl.when(jnp.logical_not(jnp.min(var - 0.01 * mean * mean) >= 0.0))
    def _():
        centred = jnp.square(x_ref[...] - stats[0:1])
        _, var = means(total, jnp.sum(centred, axis=0, keepdims=True))
        spread_out(mean, var)

    return stats[0:1], stats[1:2]


def safe_head(j, pair, half, q_ref, k_ref, v_ref):
    lanes = pl.ds(pair * 128, 128)
    query = q_ref[j, :, lanes]
    lane = lax.broadcasted_iota(jnp.int32, query.shape, 1)
    query = jnp.where((lane // HEAD) == half, query.astype(F32), 0.0).astype(BF16)
    scores = lax.dot_general(
        query, k_ref[j, :, lanes], (((1,), (1,)), ((), ())), preferred_element_type=F32
    )
    expo = jnp.exp(scores - jnp.max(scores, axis=1, keepdims=True))
    probs = (expo / jnp.sum(expo, axis=1, keepdims=True)).astype(BF16)
    return dot(probs, v_ref[j, :, lanes])


def weight_copies(weights, buffers, sems):
    wq, wk, wv, wo, _, wp = weights

    def block(i, j):
        src = (wq, wk, wv)[i]
        return pltpu.make_async_copy(
            src.at[:, pl.ds(pl.multiple_of(j * LANES, LANES), LANES)], buffers[i].at[j], sems.at[i, j]
        )

    last = [
        pltpu.make_async_copy(wo, buffers[3], sems.at[3, 0]),
        pltpu.make_async_copy(wp, buffers[4], sems.at[4, 0]),
    ]
    return block, last


def start_block(weights, buffers, sems, j):
    block, _ = weight_copies(weights, buffers, sems)
    for i in range(3):
        block(i, j).start()


def refine(rows, side, x_ref, weights, buffers, sems):
    cells = x_ref.shape[0]
    middle = rows * TW
    taps = weights[4]
    wq_s, wk_s, wv_s, wo_s, wp_s, normed, q_ref, k_ref, v_ref, att, act, range_ref, member, spread, sums, stats = buffers
    weight_block, last = weight_copies(weights, buffers, sems)

    start_block(weights, buffers, sems, 1)
    mean, rstd = group_stats(x_ref, sums, stats, member, spread)
    normed[...] = ((x_ref[...] - mean) * rstd).astype(BF16)
    range_ref[0] = jnp.full((8, 128), 1.0, F32)
    range_ref[1] = jnp.full((8, 128), 1.0, F32)

    def heads(j, carry):
        @pl.when(j < BLOCKS - 2)
        def _():
            start_block(weights, buffers, sems, j + 2)

        @pl.when(j == BLOCKS - 2)
        def _():
            last[0].start()

        @pl.when(j == BLOCKS - 1)
        def _():
            last[1].start()

        for i in range(3):
            weight_block(i, j).wait()
        n = normed[...]
        q_ref[j] = (dot(n, wq_s[j]) * (1.0 / 8.0)).astype(BF16)
        k_ref[j] = dot(n, wk_s[j]).astype(BF16)
        v_ref[j] = dot(n, wv_s[j]).astype(BF16)
        lane = lax.broadcasted_iota(jnp.int32, (cells, 128), 1)
        low, high = range_ref[0], range_ref[1]
        for pair in range(2):
            lanes = slice(pair * 128, pair * 128 + 128)
            query = q_ref[j, :, lanes]
            key = k_ref[j, :, lanes]
            value = jnp.concatenate([v_ref[j, :, lanes], jnp.ones((cells, 128), BF16)], axis=1)
            done = []
            for half in range(2):
                mine = jnp.where((lane < HEAD) == (half == 0), query, jnp.zeros_like(query))
                scores = lax.dot_general(
                    mine, key, (((1,), (1,)), ((), ())), preferred_element_type=F32
                )
                out = dot(jnp.exp(scores).astype(BF16), value)
                total = out[:, 128:]
                low = jnp.minimum(low, jnp.min(total.reshape(cells // 8, 8, 128), axis=0))
                high = jnp.maximum(high, jnp.max(total.reshape(cells // 8, 8, 128), axis=0))
                done.append(out[:, :128] / total)
            att[:, pl.ds(pl.multiple_of(j * LANES + pair * 128, 128), 128)] = jnp.where(
                lane < HEAD, done[0], done[1]
            ).astype(BF16)
        range_ref[0] = low
        range_ref[1] = high
        return carry

    lax.fori_loop(0, BLOCKS, heads, 0)
    in_range = jnp.logical_and(jnp.min(range_ref[0]) > LOW_SUM, jnp.max(range_ref[1]) < HIGH_SUM)

    @pl.when(jnp.logical_not(in_range))
    def _():
        def again(j, carry):
            lane = lax.broadcasted_iota(jnp.int32, (cells, 128), 1)
            for pair in range(2):
                done = [safe_head(j, pair, half, q_ref, k_ref, v_ref) for half in range(2)]
                att[:, pl.ds(pl.multiple_of(j * LANES + pair * 128, 128), 128)] = jnp.where(
                    lane < HEAD, done[0], done[1]
                ).astype(BF16)
            return carry

        lax.fori_loop(0, BLOCKS, again, 0)

    sums[...] = jnp.zeros_like(sums)
    last[0].wait()
    for j in range(BLOCKS):
        block = slice(j * LANES, j * LANES + LANES)
        hidden = x_ref[:, block] + dot(att[...], wo_s[:, block])
        x_ref[:, block] = hidden
        add_sums(sums, block, hidden)

    mean, rstd = group_stats(x_ref, sums, stats, member, spread)
    second = (rows + 2) * TW
    for start, width in ((0, TW), (second, 8)) if side else ((0, TW),):
        act[pl.ds(start, width), :] = jnp.zeros((width, D), F32)
        act[pl.ds(start + (rows + 1) * width, width), :] = jnp.zeros((width, D), F32)
    half_rstd = 0.5 * rstd
    parts = ((0, 0, TW), (middle, second, 8)) if side else ((0, 0, TW),)

    def activate(i, carry):
        for start, place, width in parts:
            size = 4 * width
            at = pl.ds(pl.multiple_of(start + i * size, size), size)
            half = (x_ref[at, :] - mean) * half_rstd
            to = pl.ds(pl.multiple_of(place + width + i * size, 8), size)
            act[to, :] = half + half * jnp.tanh(half)
        return carry

    lax.fori_loop(0, rows // 4, activate, 0)

    def convolve(i, carry):
        spot = lax.broadcasted_iota(jnp.int32, (4, 8, 128), 1)
        for t in range(D // 128):
            lanes = slice(t * 128, t * 128 + 128)
            weight = [taps[n : n + 1, lanes] for n in range(9)]
            sums = [[], [], []]
            for start, place, width in parts:
                size = 4 * width
                lines = [
                    act[pl.ds(pl.multiple_of(place + i * size + d * width, 8), size), lanes]
                    for d in range(3)
                ]
                for dj in range(3):
                    part = lines[0] * weight[dj] + lines[1] * weight[3 + dj] + lines[2] * weight[6 + dj]
                    part = part.reshape(4, width // 8, 8, 128)
                    sums[dj] += [part[:, n] for n in range(width // 8)]
            left = [pltpu.roll(v, 1, 1) for v in sums[0]]
            right = [pltpu.roll(v, 7, 1) for v in sums[2]]
            count = len(left)
            mixed = []
            for n in range(count):
                before = left[n - 1] if side or n > 0 else jnp.zeros_like(left[n])
                after = right[(n + 1) % count] if side or n < count - 1 else jnp.zeros_like(left[n])
                from_left = jnp.where(spot == 0, before, left[n])
                from_right = jnp.where(spot == 7, after, right[n])
                if n == 2:
                    from_left = jnp.where(spot == M, 0.0, from_left)
                    from_right = jnp.where(spot == M - 1, 0.0, from_right)
                mixed.append(sums[1][n] + from_left + from_right)
            centre = jnp.concatenate([mixed[0][:, None], mixed[1][:, None]], axis=1).reshape(4 * TW, 128)
            normed[pl.ds(pl.multiple_of(i * 4 * TW, 4 * TW), 4 * TW), lanes] = centre.astype(BF16)
            if side:
                normed[pl.ds(pl.multiple_of(middle + i * 32, 32), 32), lanes] = (
                    mixed[2].reshape(32, 128).astype(BF16)
                )
        return carry

    lax.fori_loop(0, rows // 4, convolve, 0)
    last[1].wait()


def halves(value):
    return jnp.concatenate([value[:, : D // 2], value[:, D // 2 :]], axis=0)


def tile_kernel(
    above, own, below, left, right, sides, strips, wq, wk, wv, wo, taps, wp,
    to_left, to_right, x_ref, normed, wp_s, centre, rims, out_side, part_sems, sems, *buffers,
):
    buffers = (*buffers[:4], wp_s, normed, *buffers[4:])
    copies, start = [], 0
    for i, piece in enumerate((above, own, below)):
        size = piece.shape[0]
        copies.append(pltpu.make_async_copy(piece, centre.at[pl.ds(start, size)], part_sems.at[i]))
        start += size
    copies.append(pltpu.make_async_copy(left, rims.at[pl.ds(0, STRIP)], part_sems.at[3]))
    copies.append(pltpu.make_async_copy(right, rims.at[pl.ds(STRIP, STRIP)], part_sems.at[4]))
    for copy in copies:
        copy.start()
    weights = (wq, wk, wv, wo, taps, wp)
    start_block(weights, buffers, sems, 0)
    group_matrices(buffers[-4], buffers[-3])
    sums = buffers[-2]
    sums[...] = jnp.zeros_like(sums)
    for copy in copies:
        copy.wait()
    for j in range(BLOCKS):
        block = slice(j * LANES, j * LANES + LANES)
        value = centre[:, block].astype(F32)
        x_ref[:SENT, block] = value
        add_sums(sums, block, value)
        value = dot(sides[...], rims[:, block])
        x_ref[SENT:, block] = value
        add_sums(sums, block, value)

    refine(WH, True, x_ref, weights, buffers, sems)
    for j in range(BLOCKS):
        block = slice(j * LANES, j * LANES + LANES)
        value = x_ref[SENT:, block] + dot(normed[SENT:, :], wp_s[:, block])
        out_side[:, block] = value.astype(BF16).astype(F32)
    for a in range(N_ROW):
        first = (a + M) % N_ROW
        lines = [out_side[(8 * k + first) * 8 : (8 * k + first + 1) * 8, :] for k in range(4)]
        rim = dot(strips[...], halves(jnp.concatenate(lines, axis=0).astype(BF16))).astype(BF16)
        to_right[a * 32 : a * 32 + 32, :] = rim[:32]
        to_left[a * 32 : a * 32 + 32, :] = rim[32:]


def rest_kernel(hidden, mixed, wp, mains, main, out):
    for j in range(BLOCKS):
        block = slice(j * LANES, j * LANES + LANES)
        out[:, block] = (hidden[:SENT, block] + dot(mixed[:SENT, :], wp[:, block])).astype(BF16)
    for a in range(N_ROW):
        first = (a + M) % N_ROW
        lines = [out[(8 * k + first) * TW : (8 * k + first + 1) * TW, :] for k in range(4)]
        main[a * 128 : a * 128 + 128, :] = dot(
            mains[...], halves(jnp.concatenate(lines, axis=0))
        ).astype(BF16)


def join_kernel(place, main, from_left, from_right, out):
    for a in range(N_ROW):
        first, last = a * 128, a * 128 + 96
        rim = slice(a * 32, a * 32 + 32)
        out[first : first + 32, :] = (
            main[first : first + 32, :].astype(F32) + from_left[rim, :].astype(F32)
        ).astype(BF16)
        out[first + 32 : last, :] = main[first + 32 : last, :]
        out[last : last + 32, :] = (
            main[last : last + 32, :].astype(F32) + from_right[rim, :].astype(F32)
        ).astype(BF16)


def sub_kernel(
    place, got, gathers, packing, wq, wk, wv, wo, taps, wp,
    result, gather, local, x_ref, out, gather_sem, sems, *buffers,
):
    weights = (wq, wk, wv, wo, taps, wp)
    copy = pltpu.make_async_copy(gathers.at[place[0]], gather, gather_sem)
    copy.start()
    start_block(weights, buffers, sems, 0)
    group_matrices(buffers[-4], buffers[-3])
    sums = buffers[-2]
    sums[...] = jnp.zeros_like(sums)
    late = place[1]
    copy.wait()
    for r in range(N_ROW):
        other = jnp.clip(r + 2 * late - 1, 0, N_ROW - 1)
        edge = 1 - late if r == 0 else late if r == N_ROW - 1 else 0
        cells = jnp.concatenate(
            [got[r * 128 : r * 128 + 128, :], got[pl.ds(pl.multiple_of(other * 128, 128), 128), :]],
            axis=0,
        )
        value = dot(gather[edge], cells).astype(BF16)
        at = slice(r * 48, r * 48 + 48)
        for h in range(2):
            half = slice(h * D // 2, h * D // 2 + D // 2)
            local[at, half] = value[h * 48 : h * 48 + 48]
            wide = value[h * 48 : h * 48 + 48].astype(F32)
            x_ref[at, half] = wide
            add_sums(sums, half, wide)

    refine(TH, False, x_ref, weights, buffers, sems)
    wp_s, normed = buffers[4:6]
    for j in range(BLOCKS):
        block = slice(j * LANES, j * LANES + LANES)
        value = x_ref[:, block] + dot(normed[...], wp_s[:, block])
        dilated = value.astype(BF16).astype(F32)
        out[:, block] = (0.6 * local[:, block].astype(F32) + 0.4 * dilated).astype(BF16)
    for r in range(N_ROW):
        at = slice(r * 48, r * 48 + 48)
        cells = jnp.concatenate([out[at, t * LANES : t * LANES + LANES] for t in range(BLOCKS)], axis=0)
        packed = dot(packing[...], cells).astype(BF16)
        result[r * 128 : r * 128 + 128, :LANES] = packed[:128]
        result[r * 128 : r * 128 + 128, LANES:] = packed[128:]


def unpack_kernel(got, packing, out):
    for a in range(N_ROW):
        at = slice(a * 128, a * 128 + 128)
        cells = jnp.concatenate([got[at, :LANES], got[at, LANES:]], axis=0)
        value = lax.dot_general(
            packing[...], cells, (((0,), (0,)), ((), ())), preferred_element_type=F32
        ).astype(BF16)
        for t in range(BLOCKS):
            for i in range(PART_H):
                to = (i * N_ROW + a) * TW
                out[to : to + TW, t * LANES : t * LANES + LANES] = value[
                    t * 48 + i * TW : t * 48 + i * TW + TW
                ]


def scratch(cells, padded):
    heads = pltpu.VMEM((BLOCKS, cells, LANES), BF16)
    blocks = pltpu.VMEM((BLOCKS, D, LANES), BF16)
    square = pltpu.VMEM((D, D), BF16)
    return [
        pltpu.SemaphoreType.DMA((5, BLOCKS)),
        blocks, blocks, blocks, square, square,
        pltpu.VMEM((cells, D), BF16),
        heads, heads, heads,
        pltpu.VMEM((cells, D), BF16),
        pltpu.VMEM((padded, D), F32),
        pltpu.VMEM((2, 8, 128), F32),
        pltpu.VMEM((D, 128), BF16),
        pltpu.VMEM((128, D), BF16),
        pltpu.VMEM((16, D), F32),
        pltpu.VMEM((8, D), F32),
    ]


ANY = pl.BlockSpec(memory_space=pl.ANY)
HBM = pl.BlockSpec(memory_space=pltpu.HBM)
VMEM = pl.BlockSpec(memory_space=pltpu.VMEM)


def params(mib):
    return pltpu.CompilerParams(vmem_limit_bytes=mib * 2**20)


def tile_block(above, own, below, left, right, weights):
    shape = jax.ShapeDtypeStruct
    sems, *buffers = scratch(WIN, (WH + 2) * WW)
    to_left, to_right, hidden, mixed, w_proj = pl.pallas_call(
        tile_kernel,
        out_shape=(
            shape((2 * STRIP, D // 2), BF16),
            shape((2 * STRIP, D // 2), BF16),
            shape((WIN, D), F32),
            shape((WIN, D), BF16),
            shape((D, D), BF16),
        ),
        in_specs=[ANY] * 5 + [VMEM] * 2 + [HBM] * 4 + [VMEM, HBM],
        out_specs=(VMEM,) * 5,
        scratch_shapes=[
            pltpu.VMEM((SENT, D), BF16),
            pltpu.VMEM((SIDE, D), BF16),
            pltpu.VMEM((SIDE, D), F32),
            pltpu.SemaphoreType.DMA((5,)),
            sems,
            *buffers[:4],
            *buffers[6:],
        ],
        compiler_params=params(TILE_MIB),
        name="tile_block",
    )(above, own, below, left, right, side_matrix(), strip_matrix(), *weights)
    main = pl.pallas_call(
        rest_kernel,
        out_shape=shape((2 * SENT, D // 2), BF16),
        in_specs=[VMEM] * 4,
        out_specs=VMEM,
        scratch_shapes=[pltpu.VMEM((SENT, D), BF16)],
        compiler_params=params(REST_MIB),
        name="rest",
    )(hidden, mixed, w_proj, main_matrix())
    return main, to_left, to_right


def join(place, main, from_left, from_right):
    return pl.pallas_call(
        join_kernel,
        out_shape=jax.ShapeDtypeStruct(main.shape, BF16),
        in_specs=[pl.BlockSpec(memory_space=pltpu.SMEM)] + [VMEM] * 3,
        out_specs=VMEM,
        compiler_params=params(8),
        name="join",
    )(place, main, from_left, from_right)


def sub_block(place, got, weights):
    return pl.pallas_call(
        sub_kernel,
        out_shape=jax.ShapeDtypeStruct((DEV * 8, 2 * LANES), BF16),
        in_specs=[pl.BlockSpec(memory_space=pltpu.SMEM), VMEM, HBM, VMEM] + [HBM] * 4 + [VMEM, HBM],
        out_specs=VMEM,
        scratch_shapes=[
            pltpu.VMEM((2, 96, 256), BF16),
            pltpu.VMEM((OWN, D), BF16),
            pltpu.VMEM((OWN, D), F32),
            pltpu.VMEM((OWN, D), BF16),
            pltpu.SemaphoreType.DMA,
            *scratch(OWN, (TH + 2) * TW),
        ],
        compiler_params=params(48),
        name="sub_block",
    )(place, got, gather_matrices(), packing_matrix(), *weights)


def unpack(got):
    return pl.pallas_call(
        unpack_kernel,
        out_shape=jax.ShapeDtypeStruct((OWN, D), BF16),
        in_specs=[VMEM] * 2,
        out_specs=VMEM,
        compiler_params=params(8),
        name="unpack",
    )(got, packing_matrix())


def shift(value, axis, step):
    count = lax.axis_size(axis)
    pairs = [(i, i + step) for i in range(count) if 0 <= i + step < count]
    return lax.ppermute(value, axis, pairs)


def body(latent, w_query, w_key, w_value, w_out, depth_kernel, w_proj):
    weights = (w_query, w_key, w_value, w_out, depth_kernel, w_proj)
    row, col = lax.axis_index("row"), lax.axis_index("col")
    late = (row >= M).astype(jnp.int32)
    kind = (col >= M).astype(jnp.int32) + (col >= TW - M).astype(jnp.int32)
    place = jnp.stack([3 * late + kind, late])
    above = shift(latent[TH - M :], "row", 1)
    below = shift(latent[:M], "row", -1)
    tall = jnp.concatenate([above, latent, below], axis=0)
    left = shift(tall[:, TW - M :].reshape(STRIP, D), "col", 1)
    right = shift(tall[:, :M].reshape(STRIP, D), "col", -1)
    main, to_left, to_right = tile_block(
        above.reshape(M * TW, D), latent.reshape(OWN, D), below.reshape(M * TW, D),
        left, right, weights,
    )
    main = join(place, main, shift(to_right, "col", 1), shift(to_left, "col", -1))
    both = functools.partial(
        lax.all_to_all, axis_name=("row", "col"), split_axis=0, concat_axis=0, tiled=True
    )
    got = both(main.reshape(DEV, 8, D // 2)).reshape(2 * SENT, D // 2)
    refined = sub_block(place, got, weights)
    back = both(refined.reshape(DEV, 8, 2 * LANES)).reshape(DEV * 8, 2 * LANES)
    return unpack(back).reshape(TH, TW, D)


def solution(mesh):
    return jax.shard_map(
        body,
        mesh=mesh,
        in_specs=(P("row", "col", None), P(), P(), P(), P(), P(), P()),
        out_specs=P("row", "col", None),
        check_vma=False,
    )
```
